32 devices in a mesh: parts: 1, fsdp: 8 (over z, y), query: 4 (over x, core).
Axes of the slice: x: 2, y: 2, z: 4, core: 2. Of those that a mesh axis runs over, the one named last changes fastest.
Arguments:
- resid_in: bfloat16 [2048, 8192], P(('parts', 'fsdp'), 'query'), may hold values from -120 to 120
- resid_grad: bfloat16 [2048, 8192], P(('parts', 'fsdp'), 'query'), may hold values from -6 to 6
- query_path_grad: bfloat16 [2048, 8192], P(('parts', 'fsdp'), 'query'), may hold values from -6 to 6
- hidden_act: bfloat16 [2048, 28672], P(('parts', 'fsdp'), 'query'), may hold values from -6 to 6
- key_grad: bfloat16 [2048, 1024], P(('parts', 'fsdp'), 'query'), may hold values from -6 to 6
- value_grad: bfloat16 [2048, 1024], P(('parts', 'fsdp'), 'query'), may hold values from -6 to 6
- key_weight: bfloat16 [8192, 1024], P('query', 'fsdp'), may hold values from -0.171875 to 0.171875
- value_weight: bfloat16 [8192, 1024], P('query', 'fsdp'), may hold values from -0.171875 to 0.171875
- norm_gain: bfloat16 [8192], P('query'), may hold values from 0.099609375 to 1.8984375
- proj_attn_in: bfloat16 [64, 8192], P(None, 'query'), may hold values from -0.0625 to 0.0625
- proj_key_out: bfloat16 [64, 1024], P(None, 'query'), may hold values from -0.1875 to 0.1875
- proj_value_out: bfloat16 [64, 1024], P(None, 'query'), may hold values from -0.1875 to 0.1875
- proj_down_in: bfloat16 [64, 28672], P(None, 'query'), may hold values from -0.03125 to 0.03125
- proj_down_out: bfloat16 [64, 8192], P(None, 'query'), may hold values from -0.0625 to 0.0625
- query_grads: bfloat16 [4096, 12288], P(('fsdp', 'query')), may hold values from -0.0012207031 to 0.0012207031
- seq_counts: int32 [1], P('parts'), may hold values from 256 to 2048, as said below
Outputs:
- scores: float32 [1, 4096], P('parts', ('fsdp', 'query'))
The draws below stay inside these ranges and needn't reach their ends.
Inputs may be any that keep to these rules, and one draw needn't show every extreme that they name: `seq_counts`: in every part at least one sequence has all 2048 positions valid.
All inputs are finite; a program needn't handle non-finite values.
Results may differ from the reference program's by a relative error of at most 0.0019.
Values may be sent and summed in bfloat16 or wider, within the bound.
A program may use at most 64 MiB of HBM per device.

```python
import math
import jax
import jax.numpy as jnp
from jax import lax

D = 8192
FF = 28672
KV = 1024
RANK = 64
LEN = 2048
QUERIES = 4096
TOKENS = 2048
SEQS = 1
FEATS = 12288


def draw_seq_counts(key, part):
    key = jax.random.fold_in(key, 11)
    first, second = jax.random.split(key)
    counts = jax.random.randint(first, (SEQS,), LEN // 8, LEN + 1)
    full = jax.random.randint(second, (), 0, SEQS)
    return jnp.where(jnp.arange(SEQS) == full, LEN, counts).astype(jnp.int32)


def draw_resid_in(key, part):
    key = jax.random.fold_in(key, 23)
    keys = jax.random.split(key, 3)
    rows = jnp.exp(jax.random.uniform(keys[0], (TOKENS, 1), minval=0.0, maxval=math.log(10.0)))
    columns = jnp.exp(jax.random.uniform(keys[1], (1, D), minval=0.0, maxval=math.log(10.0)))
    columns = columns * jnp.exp(math.log(3.0) * jnp.arange(D, dtype=jnp.float32) / D)
    base = 0.7 + jnp.clip(jax.random.normal(keys[2], (TOKENS, D)), -3.3, 3.3)
    return (base * rows * columns / 10.0).astype(jnp.float32).astype(jnp.bfloat16)


def projection_weight(key):
    first, second = jax.random.split(key)
    entries = jnp.clip(jax.random.normal(first, (D, KV)), -4.0, 4.0)
    column_part = jax.random.uniform(second, (1, KV), minval=-1.5, maxval=1.5)
    return ((entries + column_part) * KV ** (-0.5)).astype(jnp.float32).astype(jnp.bfloat16)


def draw_key_weight(key, part):
    key = jax.random.fold_in(key, 31)
    return projection_weight(key)


def draw_value_weight(key, part):
    key = jax.random.fold_in(key, 37)
    return projection_weight(key)


def levels(stream_key, dims, pieces, smallest, top_value):
    loudness, own = 1.0, jax.random.fold_in(stream_key, 6)
    for axis_at, shards_of in pieces:
        steps = jnp.exp(jax.random.uniform(jax.random.fold_in(own, axis_at), (shards_of,), jnp.float32, smallest / len(pieces), top_value / len(pieces)))
        loudness = loudness * jnp.repeat(steps, dims[axis_at] // shards_of).reshape([-1 if axis == axis_at else 1 for axis in range(len(dims))])
    return loudness


def normal_values(key, dims, spread, reach, pieces=(), held_as=jnp.bfloat16):
    drawn = jax.random.normal(key, dims, jnp.float32) * spread
    if len(pieces) > 0:
        drawn = levels(key, dims, pieces, -0.22, 0.18) * drawn
    return jnp.clip(drawn, min=-reach, max=reach).astype(held_as)


def setup_inputs(seed: int = 0, part: int = 0) -> dict:
    key_list = jax.random.split(jax.random.key(seed), 17)
    part_keys = jax.random.split(jax.random.fold_in(key_list[16], part), 17)
    resid_in = draw_resid_in(jax.random.fold_in(jax.random.fold_in(key_list[16], part), 71), part)
    resid_grad = normal_values(part_keys[1], (TOKENS, D), 1.0, 6.0, ((0, 8), (1, 4)))
    query_path_grad = normal_values(part_keys[2], (TOKENS, D), 1.0, 6.0, ((0, 8), (1, 4)))
    hidden_act = normal_values(part_keys[3], (TOKENS, FF), 1.0, 6.0, ((0, 8), (1, 4)))
    key_grad = normal_values(part_keys[4], (TOKENS, KV), 1.0, 6.0, ((0, 8), (1, 4)))
    value_grad = normal_values(part_keys[5], (TOKENS, KV), 1.0, 6.0, ((0, 8), (1, 4)))
    key_weight = draw_key_weight(jax.random.fold_in(key_list[16], 71), part)
    value_weight = draw_value_weight(jax.random.fold_in(key_list[16], 71), part)
    norm_gain = jnp.clip(1.0 + 0.18 * jax.random.normal(key_list[8], (D,), jnp.float32), 0.099609375, 1.8984375).astype(jnp.bfloat16)
    proj_attn_in = normal_values(key_list[9], (RANK, D), D ** -0.5, 0.0625, ((1, 4),))
    proj_key_out = normal_values(key_list[10], (RANK, KV), KV ** -0.5, 0.1875, ((1, 4),))
    proj_value_out = normal_values(key_list[11], (RANK, KV), KV ** -0.5, 0.1875, ((1, 4),))
    proj_down_in = normal_values(key_list[12], (RANK, FF), FF ** -0.5, 0.03125, ((1, 4),))
    proj_down_out = normal_values(key_list[13], (RANK, D), D ** -0.5, 0.0625, ((1, 4),))
    query_grads = normal_values(key_list[14], (QUERIES, FEATS), (FEATS * LEN) ** -0.5, 0.0012207031, ((0, 32),))
    seq_counts = draw_seq_counts(jax.random.fold_in(jax.random.fold_in(key_list[16], part), 71), part)
    return {"resid_in": resid_in, "resid_grad": resid_grad, "query_path_grad": query_path_grad, "hidden_act": hidden_act, "key_grad": key_grad, "value_grad": value_grad, "key_weight": key_weight, "value_weight": value_weight, "norm_gain": norm_gain, "proj_attn_in": proj_attn_in, "proj_key_out": proj_key_out, "proj_value_out": proj_value_out, "proj_down_in": proj_down_in, "proj_down_out": proj_down_out, "query_grads": query_grads, "seq_counts": seq_counts}


def gram_blocks(weights_mask, outer_rows, inner_rows):
    count, groups = weights_mask.shape
    width = outer_rows.shape[1]
    scaled = (weights_mask[:, :, None] * outer_rows[:, None, :]).reshape(count, groups * width)
    block = jnp.dot(scaled.T, inner_rows, precision=lax.Precision.HIGHEST, preferred_element_type=jnp.float32)
    return block.reshape(groups, width * inner_rows.shape[1])

def reference(resid_in, resid_grad, query_path_grad, hidden_act, key_grad, value_grad, key_weight, value_weight, norm_gain, proj_attn_in, proj_key_out, proj_value_out, proj_down_in, proj_down_out, query_grads, seq_counts):
    resid_f = resid_in.astype(jnp.float32)
    gain_f = norm_gain.astype(jnp.float32)
    sum_squares = lax.optimization_barrier(jnp.sum(resid_f * resid_f, axis=1))
    inv_rms = lax.rsqrt(sum_squares / D + 1e-05)
    normed = (resid_f * inv_rms[:, None] * gain_f).astype(jnp.bfloat16)
    input_grad = query_path_grad.astype(jnp.float32) + jnp.dot(key_grad, key_weight.T, preferred_element_type=jnp.float32)
    input_grad = input_grad + jnp.dot(value_grad, value_weight.T, preferred_element_type=jnp.float32)
    scaled_grad = gain_f * input_grad
    mean_dot = lax.optimization_barrier(jnp.sum(resid_f * scaled_grad, axis=1)) / D
    cubed = inv_rms * inv_rms * inv_rms * mean_dot
    resid_back = resid_grad.astype(jnp.float32) + inv_rms[:, None] * scaled_grad - resid_f * cubed[:, None]
    attn_in = jnp.dot(normed, proj_attn_in.T, preferred_element_type=jnp.float32)
    key_out = jnp.dot(key_grad, proj_key_out.T, preferred_element_type=jnp.float32)
    value_out = jnp.dot(value_grad, proj_value_out.T, preferred_element_type=jnp.float32)
    hidden_in = jnp.dot(hidden_act, proj_down_in.T, preferred_element_type=jnp.float32)
    down_out = jnp.dot(resid_back, proj_down_out.astype(jnp.float32).T, precision=lax.Precision.HIGHEST, preferred_element_type=jnp.float32)
    positions = jnp.arange(TOKENS, dtype=jnp.int32)
    seq_index = positions // LEN
    offset = positions % LEN
    onehot = seq_index[:, None] == jnp.arange(SEQS, dtype=jnp.int32)[None, :]
    limit = lax.optimization_barrier(jnp.sum(jnp.where(onehot, seq_counts[None, :], 0), axis=1))
    weights_mask = jnp.where(onehot & (offset < limit)[:, None], 1.0, 0.0).astype(jnp.float32)
    seq_grad = jnp.concatenate([gram_blocks(weights_mask, key_out, attn_in), gram_blocks(weights_mask, value_out, attn_in), gram_blocks(weights_mask, down_out, hidden_in)], axis=1)
    return jnp.dot(seq_grad, query_grads.astype(jnp.float32).T, precision=lax.Precision.HIGHEST, preferred_element_type=jnp.float32)
```

```python
import functools

import jax
import jax.numpy as jnp
from jax import lax
from jax.experimental import pallas as pl
from jax.experimental.pallas import tpu as pltpu
from jax.sharding import PartitionSpec as P

D = 8192
LEN = 2048
MESH = pl.DeviceIdType.MESH
F32 = jnp.float32
BF16 = jnp.bfloat16


def dot_nt(left, right):
    return lax.dot_general(left, right, (((1,), (1,)), ((), ())), preferred_element_type=F32)


def gram(left, right):
    return lax.dot_general(
        left,
        right,
        (((0,), (0,)), ((), ())),
        precision=lax.Precision.HIGHEST,
        preferred_element_type=F32,
    )


def split(value):
    high = value.astype(BF16)
    return high, (value - high.astype(F32)).astype(BF16)


def kernel(
    sizes,
    x_ref,
    rg_ref,
    qpg_ref,
    hid_ref,
    kg_ref,
    vg_ref,
    kgp_ref,
    w_ref,
    gain_ref,
    pai_ref,
    pko_ref,
    pvo_ref,
    pdi_ref,
    pdo_ref,
    mask_ref,
    out_kv,
    out_d,
    wg,
    xs,
    kgs,
    early,
    pks,
    prod,
    proj,
    kv_q,
    kv_f,
    d_q,
    d_f,
    w_recv,
    w_right,
    w_left,
    x_sem,
    kg_send,
    kg_recv,
    early_sem,
    pk_sem,
    kv_q_sem,
    kv_f_sem,
    d_q_sem,
    d_f_sem,
):
    F, Q, B, seqs = sizes
    A = F // B
    per_seq = F // seqs
    n = kgp_ref.shape[1]
    t, d = x_ref.shape
    r = pdo_ref.shape[0]
    f, q = lax.axis_index("fsdp"), lax.axis_index("query")
    a, b = f // B, lax.rem(f, B)

    barrier = pltpu.get_barrier_semaphore()
    others = 0
    for i in range(1, F):
        pl.semaphore_signal(
            barrier, inc=1, device_id={"fsdp": lax.rem(f + i, F)}, device_id_type=MESH
        )
        others += 1
    for bi in range(B):
        for qi in range(1, Q):
            pl.semaphore_signal(
                barrier,
                inc=1,
                device_id={"fsdp": a * B + lax.rem(b + bi, B), "query": lax.rem(q + qi, Q)},
                device_id_type=MESH,
            )
            others += 1
    pl.semaphore_wait(barrier, others)

    right = {"fsdp": jnp.minimum(f + B, F - 1 - lax.rem(F - 1 - f, B))}
    left = {"fsdp": jnp.maximum(f - B, b)}
    has_right, has_left = a < A - 1, a > 0

    def w_copy(src, slot, send, target):
        return pltpu.make_async_remote_copy(
            src_ref=src,
            dst_ref=wg.at[slot],
            send_sem=send.at[slot],
            recv_sem=w_recv.at[slot],
            device_id=target,
            device_id_type=MESH,
        )

    @pl.when(has_right)
    def _():
        w_copy(w_ref, a, w_right, right).start()

    @pl.when(has_left)
    def _():
        w_copy(w_ref, a, w_left, left).start()

    gain = gain_ref[...].astype(F32)
    own = pl.ds(pl.multiple_of(b * t, t), t)
    xs[own, :] = (x_ref[...].astype(F32) * gain).astype(BF16)
    gp_high, gp_low = split(pdo_ref[...].astype(F32) * gain)
    xs[pl.ds(B * t, r), :] = gp_high
    xs[pl.ds(B * t + r, r), :] = gp_low

    waits = []
    for bi in range(1, B):
        there = lax.rem(b + bi, B)
        copy = pltpu.make_async_remote_copy(
            src_ref=xs.at[own, :],
            dst_ref=xs.at[own, :],
            send_sem=x_sem.at[0, bi],
            recv_sem=x_sem.at[1, bi],
            device_id={"fsdp": a * B + there},
            device_id_type=MESH,
        )
        copy.start()
        waits.append(copy)
    kgs[pl.ds(q * n, n), own, :] = kgp_ref[b]
    for bi in range(B):
        for qi in range(Q):
            if bi == 0 and qi == 0:
                continue
            there = lax.rem(b + bi, B)
            copy = pltpu.make_async_remote_copy(
                src_ref=kgp_ref.at[there],
                dst_ref=kgs.at[pl.ds(q * n, n), own, :],
                send_sem=kg_send.at[bi, qi],
                recv_sem=kg_recv.at[bi, qi],
                device_id={"fsdp": a * B + there, "query": lax.rem(q + qi, Q)},
                device_id_type=MESH,
            )
            copy.start()
            waits.append(copy)

    def spread(buffer, sems, axis, me, count):
        copies = []
        for i in range(1, count):
            copy = pltpu.make_async_remote_copy(
                src_ref=buffer.at[me],
                dst_ref=buffer.at[me],
                send_sem=sems.at[0, i],
                recv_sem=sems.at[1, i],
                device_id={axis: lax.rem(me + i, count)},
                device_id_type=MESH,
            )
            copy.start()
            copies.append(copy)
        return copies

    x = x_ref[...]
    xf = x.astype(F32)
    early[q, :, pl.ds(0, r)] = dot_nt(kg_ref[...], pko_ref[...])
    early[q, :, pl.ds(r, r)] = dot_nt(vg_ref[...], pvo_ref[...])
    early[q, :, pl.ds(2 * r, r)] = dot_nt(hid_ref[...], pdi_ref[...])
    early[q, :, pl.ds(3 * r, r)] = dot_nt(x, pdo_ref[...])
    early[q, :, pl.ds(4 * r, 2 * r)] = jnp.broadcast_to(
        jnp.sum(xf * xf, axis=1, keepdims=True), (t, 2 * r)
    )
    early_copies = spread(early, early_sem, "query", q, Q)
    qpg = qpg_ref[...]
    md0 = jnp.sum(xf * gain * qpg.astype(F32), axis=1, keepdims=True) / D
    rg_out = dot_nt(rg_ref[...], pdo_ref[...])
    qpg_out = dot_nt(qpg, xs[pl.ds(B * t, r), :]) + dot_nt(qpg, xs[pl.ds(B * t + r, r), :])
    for copy in early_copies:
        copy.wait()
    whole = early[0]
    for i in range(1, Q):
        whole = whole + early[i]
    mask = mask_ref[...]
    inv = lax.rsqrt(whole[:, 4 * r :] / D + 1e-05)
    inv_col = inv[:, :1]
    inv_r = inv[:, :r]
    cubed = inv_r * inv_r * inv_r
    back = whole[:, 3 * r : 4 * r] * cubed
    hidden = whole[:, 2 * r : 3 * r] * mask[:, :r]
    pks[own, pl.ds(0, r)] = hidden
    pks[own, pl.ds(r, r)] = back
    pks[own, pl.ds(2 * r, 2 * r)] = inv
    for bi in range(1, B):
        copy = pltpu.make_async_remote_copy(
            src_ref=pks.at[own, :],
            dst_ref=pks.at[own, :],
            send_sem=pk_sem.at[0, bi],
            recv_sem=pk_sem.at[1, bi],
            device_id={"fsdp": a * B + lax.rem(b + bi, B)},
            device_id_type=MESH,
        )
        copy.start()
        waits.append(copy)
    normed = (xf * inv_col * gain).astype(BF16)
    attn = dot_nt(normed, pai_ref[...])
    kv_q[q, :, pl.ds(0, r)] = gram(whole[:, :r] * mask[:, :r], attn)
    kv_q[q, :, pl.ds(r, r)] = gram(whole[:, r : 2 * r] * mask[:, :r], attn)
    kv_copies = spread(kv_q, kv_q_sem, "query", q, Q)
    down0 = gram(rg_out + inv_r * qpg_out - back * md0, hidden)

    prod[...] = jnp.zeros_like(prod)
    proj[...] = jnp.zeros_like(proj)
    for copy in kv_copies:
        copy.wait()
    total = kv_q[0]
    for i in range(1, Q):
        total = total + kv_q[i]
    kv_f[f] = total
    kv_copies = spread(kv_f, kv_f_sem, "fsdp", f, F)
    for copy in waits:
        copy.wait()

    def block(weights, slot):
        y = jnp.dot(xs[...], weights, preferred_element_type=F32)
        cols = kgs[slot]
        prod[...] += y[: B * t] * cols.astype(F32)
        high, low = split(y[B * t : B * t + r] + y[B * t + r :])
        proj[...] += dot_nt(cols, high) + dot_nt(cols, low)

    block(w_ref[...], a)

    def step(s, carry):
        before, after = a - s, a + s

        @pl.when(before >= 0)
        def _():
            w_copy(w_ref, before, w_left, left).wait_recv()

        @pl.when((before >= 0) & has_right)
        def _():
            w_copy(wg.at[before], before, w_right, right).start()

        @pl.when(after < A)
        def _():
            w_copy(w_ref, after, w_right, right).wait_recv()

        @pl.when((after < A) & has_left)
        def _():
            w_copy(wg.at[after], after, w_left, left).start()

        @pl.when(before >= 0)
        def _():
            block(wg[before], before)

        @pl.when(after < A)
        def _():
            block(wg[after], after)

        return carry

    lax.fori_loop(1, A, step, 0)

    dots = jnp.sum(prod[...], axis=1, keepdims=True) / D
    packed = pks[...]
    late = packed[:, 2 * r : 3 * r] * proj[...] - packed[:, r : 2 * r] * dots
    d_q[q] = down0 + gram(late, packed[:, :r])
    for copy in spread(d_q, d_q_sem, "query", q, Q):
        copy.wait()
    total = d_q[0]
    for i in range(1, Q):
        total = total + d_q[i]
    d_f[f] = total
    d_copies = spread(d_f, d_f_sem, "fsdp", f, F)

    def drain(slot, carry):
        @pl.when((slot <= a) & has_right)
        def _():
            w_copy(w_ref, slot, w_right, right).wait_send()

        @pl.when((slot >= a) & has_left)
        def _():
            w_copy(w_ref, slot, w_left, left).wait_send()

        return carry

    lax.fori_loop(0, A, drain, 0)
    for copy in kv_copies:
        copy.wait()
    for buffer, out, copies in ((kv_f, out_kv, ()), (d_f, out_d, d_copies)):
        for copy in copies:
            copy.wait()
        for seq in range(seqs):
            total = buffer[seq * per_seq]
            for i in range(1, per_seq):
                total = total + buffer[seq * per_seq + i]
            out[seq] = total


def shards(
    F,
    Q,
    resid_in,
    resid_grad,
    query_path_grad,
    hidden_act,
    key_grad,
    value_grad,
    key_weight,
    value_weight,
    norm_gain,
    proj_attn_in,
    proj_key_out,
    proj_value_out,
    proj_down_in,
    proj_down_out,
    query_grads,
    seq_counts,
):
    B = 2
    A = F // B
    t, d = resid_in.shape
    w = key_weight.shape[1]
    r = proj_attn_in.shape[0]
    seqs = seq_counts.shape[0]
    n = key_grad.shape[1] // (w * B)
    fsdp_place = lax.axis_index("fsdp")

    def by_side(grad):
        return grad.reshape(t, n, B, w).transpose(2, 1, 0, 3)

    kgp = jnp.concatenate([by_side(key_grad), by_side(value_grad)], axis=3)
    weights = jnp.concatenate([key_weight, value_weight], axis=1)
    positions = fsdp_place * t + lax.iota(jnp.int32, t)
    limit = jnp.sum(
        jnp.where(
            (positions // LEN)[:, None] == lax.iota(jnp.int32, seqs)[None, :], seq_counts[None, :], 0
        ),
        axis=1,
    )
    mask = jnp.where(positions % LEN < limit, 1.0, 0.0).astype(F32)
    mask = jnp.broadcast_to(mask[:, None], (t, 2 * r))

    vmem = pl.BlockSpec(memory_space=pltpu.VMEM)
    dma = pltpu.SemaphoreType.DMA
    out_kv, out_d = pl.pallas_call(
        functools.partial(kernel, (F, Q, B, seqs)),
        out_shape=(
            jax.ShapeDtypeStruct((seqs, r, 2 * r), F32),
            jax.ShapeDtypeStruct((seqs, r, r), F32),
        ),
        in_specs=[vmem] * 15,
        out_specs=(vmem, vmem),
        scratch_shapes=[
            pltpu.VMEM((A, d, 2 * w), BF16),
            pltpu.VMEM((B * t + 2 * r, d), BF16),
            pltpu.VMEM((A, B * t, 2 * w), BF16),
            pltpu.VMEM((Q, t, 6 * r), F32),
            pltpu.VMEM((B * t, 4 * r), F32),
            pltpu.VMEM((B * t, 2 * w), F32),
            pltpu.VMEM((B * t, r), F32),
            pltpu.VMEM((Q, r, 2 * r), F32),
            pltpu.VMEM((F, r, 2 * r), F32),
            pltpu.VMEM((Q, r, r), F32),
            pltpu.VMEM((F, r, r), F32),
            dma((A,)),
            dma((A,)),
            dma((A,)),
            dma((2, B)),
            dma((B, Q)),
            dma((B, Q)),
            dma((2, Q)),
            dma((2, B)),
            dma((2, Q)),
            dma((2, F)),
            dma((2, Q)),
            dma((2, F)),
        ],
        compiler_params=pltpu.CompilerParams(
            collective_id=0, has_side_effects=True, vmem_limit_bytes=50 * 2**20
        ),
    )(
        resid_in,
        resid_grad,
        query_path_grad,
        hidden_act,
        key_grad,
        value_grad,
        kgp,
        weights,
        norm_gain.reshape(1, d),
        proj_attn_in,
        proj_key_out,
        proj_value_out,
        proj_down_in,
        proj_down_out,
        mask,
    )
    seq_grad = jnp.concatenate(
        [
            out_kv[:, :, :r].reshape(seqs, r * r),
            out_kv[:, :, r:].reshape(seqs, r * r),
            out_d.reshape(seqs, r * r),
        ],
        axis=1,
    )
    return jnp.dot(
        seq_grad,
        query_grads.astype(F32).T,
        precision=lax.Precision.HIGHEST,
        preferred_element_type=F32,
    )


def solution(mesh):
    placed = (
        P(("parts", "fsdp"), "query"),
        P(("parts", "fsdp"), "query"),
        P(("parts", "fsdp"), "query"),
        P(("parts", "fsdp"), "query"),
        P(("parts", "fsdp"), "query"),
        P(("parts", "fsdp"), "query"),
        P("query", "fsdp"),
        P("query", "fsdp"),
        P("query"),
        P(None, "query"),
        P(None, "query"),
        P(None, "query"),
        P(None, "query"),
        P(None, "query"),
        P(("fsdp", "query"), None),
        P("parts"),
    )
    return jax.shard_map(
        functools.partial(shards, mesh.shape["fsdp"], mesh.shape["query"]),
        mesh=mesh,
        in_specs=placed,
        out_specs=P("parts", ("fsdp", "query")),
        check_vma=False,
    )
```

```python
import functools

import jax
import jax.numpy as jnp
from jax import lax
from jax.experimental import pallas as pl
from jax.experimental.pallas import tpu as pltpu
from jax.sharding import PartitionSpec as P

D = 8192
LEN = 2048
MESH = pl.DeviceIdType.MESH
F32 = jnp.float32
BF16 = jnp.bfloat16


def dot_nt(left, right):
    return lax.dot_general(left, right, (((1,), (1,)), ((), ())), preferred_element_type=F32)


def gram(left, right):
    return lax.dot_general(
        left,
        right,
        (((0,), (0,)), ((), ())),
        precision=lax.Precision.HIGHEST,
        preferred_element_type=F32,
    )


def split(value):
    high = value.astype(BF16)
    return high, (value - high.astype(F32)).astype(BF16)


def kernel(
    sizes,
    x_ref,
    rg_hbm,
    qpg_hbm,
    hid_hbm,
    kg_ref,
    vg_ref,
    wk_hbm,
    wv_hbm,
    gain_ref,
    pai_ref,
    pko_ref,
    pvo_ref,
    pdi_hbm,
    pdo_ref,
    grads_hbm,
    counts_ref,
    out_ref,
    rg_ref,
    qpg_ref,
    hid_ref,
    pdi_ref,
    grads_ref,
    wg,
    xs,
    kgp_ref,
    kgs,
    early,
    pks,
    prod,
    proj,
    kv_q,
    kv_f,
    d_q,
    d_f,
    flat,
    load_sem,
    w_recv,
    w_right,
    w_left,
    x_sem,
    kg_send,
    kg_recv,
    early_sem,
    pk_sem,
    kv_q_sem,
    kv_f_sem,
    d_q_sem,
    d_f_sem,
):
    F, Q, B, seqs = sizes
    A = F // B
    per_seq = F // seqs
    n = kgp_ref.shape[1]
    t, d = x_ref.shape
    w = wk_hbm.shape[1]
    r = pdo_ref.shape[0]
    f, q = lax.axis_index("fsdp"), lax.axis_index("query")
    a, b = f // B, lax.rem(f, B)

    barrier = pltpu.get_barrier_semaphore()
    others = 0
    for i in range(1, F):
        pl.semaphore_signal(
            barrier, inc=1, device_id={"fsdp": lax.rem(f + i, F)}, device_id_type=MESH
        )
        others += 1
    for bi in range(B):
        for qi in range(1, Q):
            pl.semaphore_signal(
                barrier,
                inc=1,
                device_id={"fsdp": a * B + lax.rem(b + bi, B), "query": lax.rem(q + qi, Q)},
                device_id_type=MESH,
            )
            others += 1

    loads = [
        pltpu.make_async_copy(src, dst, load_sem.at[i])
        for i, (src, dst) in enumerate(
            (
                (hid_hbm, hid_ref),
                (pdi_hbm, pdi_ref),
                (qpg_hbm, qpg_ref),
                (rg_hbm, rg_ref),
                (wk_hbm, wg.at[a, 0]),
                (wv_hbm, wg.at[a, 1]),
                (grads_hbm, grads_ref),
            )
        )
    ]
    for load in loads:
        load.start()
    gain = gain_ref[...].astype(F32)
    own = pl.ds(pl.multiple_of(b * t, t), t)
    xs[own, :] = (x_ref[...].astype(F32) * gain).astype(BF16)
    gp_high, gp_low = split(pdo_ref[...].astype(F32) * gain)
    xs[pl.ds(B * t, r), :] = gp_high
    xs[pl.ds(B * t + r, r), :] = gp_low
    for bi in range(B):
        for i in range(n):
            at = (i * B + bi) * w
            kgp_ref[bi, i, :, pl.ds(0, w)] = kg_ref[:, at : at + w]
            kgp_ref[bi, i, :, pl.ds(w, w)] = vg_ref[:, at : at + w]
    pl.semaphore_wait(barrier, others)

    right = {"fsdp": jnp.minimum(f + B, F - 1 - lax.rem(F - 1 - f, B))}
    left = {"fsdp": jnp.maximum(f - B, b)}
    has_right, has_left = a < A - 1, a > 0

    def w_copy(src, slot, part, send, target):
        return pltpu.make_async_remote_copy(
            src_ref=src,
            dst_ref=wg.at[slot, part],
            send_sem=send.at[slot, part],
            recv_sem=w_recv.at[slot, part],
            device_id=target,
            device_id_type=MESH,
        )

    for part, source in enumerate((wk_hbm, wv_hbm)):

        @pl.when(has_right)
        def _():
            w_copy(source, a, part, w_right, right).start()

        @pl.when(has_left)
        def _():
            w_copy(source, a, part, w_left, left).start()

    waits = []
    kgs[pl.ds(q * n, n), own, :] = kgp_ref[b]
    for bi in range(B):
        for qi in range(Q):
            if bi == 0 and qi == 0:
                continue
            there = lax.rem(b + bi, B)
            copy = pltpu.make_async_remote_copy(
                src_ref=kgp_ref.at[there],
                dst_ref=kgs.at[pl.ds(q * n, n), own, :],
                send_sem=kg_send.at[bi, qi],
                recv_sem=kg_recv.at[bi, qi],
                device_id={"fsdp": a * B + there, "query": lax.rem(q + qi, Q)},
                device_id_type=MESH,
            )
            copy.start()
            waits.append(copy)
    for bi in range(1, B):
        there = lax.rem(b + bi, B)
        copy = pltpu.make_async_remote_copy(
            src_ref=xs.at[own, :],
            dst_ref=xs.at[own, :],
            send_sem=x_sem.at[0, bi],
            recv_sem=x_sem.at[1, bi],
            device_id={"fsdp": a * B + there},
            device_id_type=MESH,
        )
        copy.start()
        waits.append(copy)

    def spread(buffer, sems, axis, me, count):
        copies = []
        for i in range(1, count):
            copy = pltpu.make_async_remote_copy(
                src_ref=buffer.at[me],
                dst_ref=buffer.at[me],
                send_sem=sems.at[0, i],
                recv_sem=sems.at[1, i],
                device_id={axis: lax.rem(me + i, count)},
                device_id_type=MESH,
            )
            copy.start()
            copies.append(copy)
        return copies

    def forward(s):
        before, after = a - s, a + s
        for part in range(2):

            @pl.when(before >= 0)
            def _():
                w_copy(wg.at[before, part], before, part, w_left, left).wait_recv()

            @pl.when((before >= 0) & has_right)
            def _():
                w_copy(wg.at[before, part], before, part, w_right, right).start()

            @pl.when(after < A)
            def _():
                w_copy(wg.at[after, part], after, part, w_right, right).wait_recv()

            @pl.when((after < A) & has_left)
            def _():
                w_copy(wg.at[after, part], after, part, w_left, left).start()

    def block(slot):
        weights = jnp.concatenate([wg[slot, 0], wg[slot, 1]], axis=1)
        y = jnp.dot(xs[...], weights, preferred_element_type=F32)
        cols = kgs[slot]
        prod[...] += y[: B * t] * cols.astype(F32)
        high, low = split(y[B * t : B * t + r] + y[B * t + r :])
        proj[...] += dot_nt(cols, high) + dot_nt(cols, low)

    def contract(s):
        @pl.when(a - s >= 0)
        def _():
            block(a - s)

        @pl.when(a + s < A)
        def _():
            block(a + s)

    x = x_ref[...]
    xf = x.astype(F32)
    early[q, :, pl.ds(0, r)] = dot_nt(kg_ref[...], pko_ref[...])
    early[q, :, pl.ds(r, r)] = dot_nt(vg_ref[...], pvo_ref[...])
    early[q, :, pl.ds(3 * r, r)] = dot_nt(x, pdo_ref[...])
    early[q, :, pl.ds(4 * r, 2 * r)] = jnp.broadcast_to(
        jnp.sum(xf * xf, axis=1, keepdims=True), (t, 2 * r)
    )
    for load in loads:
        load.wait()
    early[q, :, pl.ds(2 * r, r)] = dot_nt(hid_ref[...], pdi_ref[...])
    early_copies = spread(early, early_sem, "query", q, Q)
    qpg = qpg_ref[...]
    md0 = jnp.sum(xf * gain * qpg.astype(F32), axis=1, keepdims=True) / D
    rg_out = dot_nt(rg_ref[...], pdo_ref[...])
    qpg_out = dot_nt(qpg, xs[pl.ds(B * t, r), :]) + dot_nt(qpg, xs[pl.ds(B * t + r, r), :])
    prod[...] = jnp.zeros_like(prod)
    proj[...] = jnp.zeros_like(proj)

    forward(1)
    for copy in early_copies:
        copy.wait()
    whole = early[0]
    for i in range(1, Q):
        whole = whole + early[i]
    place = f // per_seq
    limit = jnp.int32(0)
    for seq in range(seqs):
        limit += jnp.where(place == seq, counts_ref[seq], 0)
    position = lax.rem(f, per_seq) * t + lax.broadcasted_iota(jnp.int32, (t, r), 0)
    mask = jnp.where(position < limit, 1.0, 0.0).astype(F32)
    inv = lax.rsqrt(whole[:, 4 * r :] / D + 1e-05)
    inv_col = inv[:, :1]
    inv_r = inv[:, :r]
    cubed = inv_r * inv_r * inv_r
    back = whole[:, 3 * r : 4 * r] * cubed
    hidden = whole[:, 2 * r : 3 * r] * mask
    pks[own, pl.ds(0, r)] = hidden
    pks[own, pl.ds(r, r)] = back
    pks[own, pl.ds(2 * r, 2 * r)] = inv
    for bi in range(1, B):
        copy = pltpu.make_async_remote_copy(
            src_ref=pks.at[own, :],
            dst_ref=pks.at[own, :],
            send_sem=pk_sem.at[0, bi],
            recv_sem=pk_sem.at[1, bi],
            device_id={"fsdp": a * B + lax.rem(b + bi, B)},
            device_id_type=MESH,
        )
        copy.start()
        waits.append(copy)
    normed = (xf * inv_col * gain).astype(BF16)
    attn = dot_nt(normed, pai_ref[...])
    kv_q[q, :, pl.ds(0, r)] = gram(whole[:, :r] * mask, attn)
    kv_q[q, :, pl.ds(r, r)] = gram(whole[:, r : 2 * r] * mask, attn)
    kv_copies = spread(kv_q, kv_q_sem, "query", q, Q)
    down0 = gram(rg_out + inv_r * qpg_out - back * md0, hidden)

    if A > 2:
        forward(2)
    for copy in waits:
        copy.wait()
    for copy in kv_copies:
        copy.wait()
    total = kv_q[0]
    for i in range(1, Q):
        total = total + kv_q[i]
    kv_f[f] = total
    kv_copies = spread(kv_f, kv_f_sem, "fsdp", f, F)
    block(a)
    contract(1)

    def step(s, carry):
        forward(s)
        contract(s - 1)
        return carry

    def by_query(total, at):
        for seq in range(seqs):
            for i in range(r):
                flat[seq, pl.ds(0, 1), pl.ds(at + i * r, r)] = total[seq][i : i + 1, :]

    def score(start, size):
        grads = grads_ref[:, start : start + size]
        parts = []
        for seq in range(seqs):
            row = jnp.broadcast_to(flat[seq, pl.ds(0, 1), pl.ds(start, size)], (16, size))
            high = row.astype(BF16)
            rest = row - high.astype(F32)
            middle = rest.astype(BF16)
            low = (rest - middle.astype(F32)).astype(BF16)
            value = dot_nt(high, grads) + (dot_nt(middle, grads) + dot_nt(low, grads))
            parts.append(value[:1])
        return parts

    def sequences(buffer):
        totals = []
        for seq in range(seqs):
            total = buffer[seq * per_seq]
            for i in range(1, per_seq):
                total = total + buffer[seq * per_seq + i]
            totals.append(total)
        return totals

    if A > 2:
        lax.fori_loop(3, A, step, 0)
    for copy in kv_copies:
        copy.wait()
    totals = sequences(kv_f)
    by_query([total[:, :r] for total in totals], 0)
    by_query([total[:, r:] for total in totals], r * r)
    scores = score(0, 2 * r * r)
    if A > 2:
        contract(A - 1)

    dots = jnp.sum(prod[...], axis=1, keepdims=True) / D
    packed = pks[...]
    late = packed[:, 2 * r : 3 * r] * proj[...] - packed[:, r : 2 * r] * dots
    d_q[q] = down0 + gram(late, packed[:, :r])
    for copy in spread(d_q, d_q_sem, "query", q, Q):
        copy.wait()
    total = d_q[0]
    for i in range(1, Q):
        total = total + d_q[i]
    d_f[f] = total
    d_copies = spread(d_f, d_f_sem, "fsdp", f, F)

    def drain(slot, carry):
        for part in range(2):

            @pl.when((slot <= a) & has_right)
            def _():
                w_copy(wg.at[slot, part], slot, part, w_right, right).wait_send()

            @pl.when((slot >= a) & has_left)
            def _():
                w_copy(wg.at[slot, part], slot, part, w_left, left).wait_send()

        return carry

    lax.fori_loop(0, A, drain, 0)
    for copy in d_copies:
        copy.wait()
    by_query(sequences(d_f), 2 * r * r)
    for seq, late_scores in enumerate(score(2 * r * r, r * r)):
        out_ref[pl.ds(seq, 1), :] = scores[seq] + late_scores


def shards(
    F,
    Q,
    resid_in,
    resid_grad,
    query_path_grad,
    hidden_act,
    key_grad,
    value_grad,
    key_weight,
    value_weight,
    norm_gain,
    proj_attn_in,
    proj_key_out,
    proj_value_out,
    proj_down_in,
    proj_down_out,
    query_grads,
    seq_counts,
):
    B = 2
    A = F // B
    t, d = resid_in.shape
    w = key_weight.shape[1]
    r = proj_attn_in.shape[0]
    seqs = seq_counts.shape[0]
    n = key_grad.shape[1] // (w * B)
    vmem = pl.BlockSpec(memory_space=pltpu.VMEM)
    hbm = pl.BlockSpec(memory_space=pl.ANY)
    dma = pltpu.SemaphoreType.DMA
    operands = (
        (resid_in, vmem),
        (resid_grad, hbm),
        (query_path_grad, hbm),
        (hidden_act, hbm),
        (key_grad, vmem),
        (value_grad, vmem),
        (key_weight, hbm),
        (value_weight, hbm),
        (norm_gain.reshape(1, d), vmem),
        (proj_attn_in, vmem),
        (proj_key_out, vmem),
        (proj_value_out, vmem),
        (proj_down_in, hbm),
        (proj_down_out, vmem),
        (query_grads, hbm),
        (seq_counts, pl.BlockSpec(memory_space=pltpu.SMEM)),
    )
    return pl.pallas_call(
        functools.partial(kernel, (F, Q, B, seqs)),
        out_shape=jax.ShapeDtypeStruct((seqs, query_grads.shape[0]), F32),
        in_specs=[spec for _, spec in operands],
        out_specs=vmem,
        scratch_shapes=[
            pltpu.VMEM(resid_grad.shape, BF16),
            pltpu.VMEM(query_path_grad.shape, BF16),
            pltpu.VMEM(hidden_act.shape, BF16),
            pltpu.VMEM(proj_down_in.shape, BF16),
            pltpu.VMEM(query_grads.shape, BF16),
            pltpu.VMEM((A, 2, d, w), BF16),
            pltpu.VMEM((B * t + 2 * r, d), BF16),
            pltpu.VMEM((B, n, t, 2 * w), BF16),
            pltpu.VMEM((A, B * t, 2 * w), BF16),
            pltpu.VMEM((Q, t, 6 * r), F32),
            pltpu.VMEM((B * t, 4 * r), F32),
            pltpu.VMEM((B * t, 2 * w), F32),
            pltpu.VMEM((B * t, r), F32),
            pltpu.VMEM((Q, r, 2 * r), F32),
            pltpu.VMEM((F, r, 2 * r), F32),
            pltpu.VMEM((Q, r, r), F32),
            pltpu.VMEM((F, r, r), F32),
            pltpu.VMEM((seqs, 8, 3 * r * r), F32),
            dma((7,)),
            dma((A, 2)),
            dma((A, 2)),
            dma((A, 2)),
            dma((2, B)),
            dma((B, Q)),
            dma((B, Q)),
            dma((2, Q)),
            dma((2, B)),
            dma((2, Q)),
            dma((2, F)),
            dma((2, Q)),
            dma((2, F)),
        ],
        compiler_params=pltpu.CompilerParams(
            collective_id=0, has_side_effects=True, vmem_limit_bytes=56 * 2**20
        ),
    )(*(operand for operand, _ in operands))


def solution(mesh):
    placed = (
        P(("parts", "fsdp"), "query"),
        P(("parts", "fsdp"), "query"),
        P(("parts", "fsdp"), "query"),
        P(("parts", "fsdp"), "query"),
        P(("parts", "fsdp"), "query"),
        P(("parts", "fsdp"), "query"),
        P("query", "fsdp"),
        P("query", "fsdp"),
        P("query"),
        P(None, "query"),
        P(None, "query"),
        P(None, "query"),
        P(None, "query"),
        P(None, "query"),
        P(("fsdp", "query"), None),
        P("parts"),
    )
    return jax.shard_map(
        functools.partial(shards, mesh.shape["fsdp"], mesh.shape["query"]),
        mesh=mesh,
        in_specs=placed,
        out_specs=P("parts", ("fsdp", "query")),
        check_vma=False,
    )
```

```python
import functools

import jax
import jax.numpy as jnp
from jax import lax
from jax.experimental import pallas as pl
from jax.experimental.pallas import tpu as pltpu
from jax.sharding import PartitionSpec as P

D = 8192
LEN = 2048
CHUNKS = 4
MESH = pl.DeviceIdType.MESH
F32 = jnp.float32
BF16 = jnp.bfloat16


def dot_nt(left, right):
    return lax.dot_general(left, right, (((1,), (1,)), ((), ())), preferred_element_type=F32)


def gram(left, right):
    return lax.dot_general(
        left,
        right,
        (((0,), (0,)), ((), ())),
        precision=lax.Precision.HIGHEST,
        preferred_element_type=F32,
    )


def split(value):
    high = value.astype(BF16)
    return high, (value - high.astype(F32)).astype(BF16)


def kernel(
    sizes,
    x_ref,
    rg_hbm,
    qpg_hbm,
    hid_hbm,
    kg_ref,
    vg_ref,
    wk_hbm,
    wv_hbm,
    gain_ref,
    pai_ref,
    pko_ref,
    pvo_ref,
    pdi_hbm,
    pdo_ref,
    grads_hbm,
    counts_ref,
    out_ref,
    rg_ref,
    qpg_ref,
    hid_ref,
    pdi_ref,
    grads_ref,
    wg,
    xs,
    kgp_ref,
    kgs,
    early,
    pks,
    prod,
    proj,
    kv_q,
    kv_f,
    d_q,
    d_f,
    flat,
    load_sem,
    w_recv,
    w_right,
    w_left,
    x_sem,
    x_end_sem,
    x_extra_sem,
    kg_pair_sem,
    kg_sem,
    kg_end_sem,
    kg_extra_sem,
    early_sem,
    pk_sem,
    pk_end_sem,
    pk_extra_sem,
    kv_q_sem,
    kv_f_sem,
    d_q_sem,
    d_f_sem,
):
    F, Q, B, seqs = sizes
    A = F // B
    per_seq = F // seqs
    n = kgp_ref.shape[1]
    t, d = x_ref.shape
    w = wk_hbm.shape[1]
    r = pdo_ref.shape[0]
    f, q = lax.axis_index("fsdp"), lax.axis_index("query")
    a, b = f // B, lax.rem(f, B)

    barrier = pltpu.get_barrier_semaphore()
    others = 0
    for i in range(1, F):
        pl.semaphore_signal(
            barrier, inc=1, device_id={"fsdp": lax.rem(f + i, F)}, device_id_type=MESH
        )
        others += 1
    for qi in range(1, Q):
        pl.semaphore_signal(
            barrier, inc=1, device_id={"query": lax.rem(q + qi, Q)}, device_id_type=MESH
        )
        others += 1

    loads = [
        pltpu.make_async_copy(src, dst, load_sem.at[i])
        for i, (src, dst) in enumerate(
            (
                (hid_hbm, hid_ref),
                (pdi_hbm, pdi_ref),
                (qpg_hbm, qpg_ref),
                (rg_hbm, rg_ref),
                (wk_hbm, wg.at[a, 0]),
                (wv_hbm, wg.at[a, 1]),
                (grads_hbm, grads_ref),
            )
        )
    ]
    for load in loads:
        load.start()
    gain = gain_ref[...].astype(F32)
    own = pl.ds(pl.multiple_of(b * t, t), t)
    xs[own, :] = (x_ref[...].astype(F32) * gain).astype(BF16)
    gp_high, gp_low = split(pdo_ref[...].astype(F32) * gain)
    xs[pl.ds(B * t, r), :] = gp_high
    xs[pl.ds(B * t + r, r), :] = gp_low
    for bi in range(B):
        for i in range(n):
            at = (i * B + bi) * w
            kgp_ref[bi, i, :, pl.ds(0, w)] = kg_ref[:, at : at + w]
            kgp_ref[bi, i, :, pl.ds(w, w)] = vg_ref[:, at : at + w]
    pl.semaphore_wait(barrier, others)

    right = {"fsdp": jnp.minimum(f + B, F - 1 - lax.rem(F - 1 - f, B))}
    left = {"fsdp": jnp.maximum(f - B, b)}
    is_end = (a == 0) | (a == A - 1)
    is_host = (a > 0) & (a < A - 1)
    has_extra = (a == 1) | (a == A - 2)
    inward = {"fsdp": jnp.where(a == 0, f + B, f - B)}
    has_right, has_left = a < A - 2, a > 1
    extra = B * t + 2 * r
    piece = t // CHUNKS

    def remote(src, dst, sems, at, target):
        return pltpu.make_async_remote_copy(
            src_ref=src,
            dst_ref=dst,
            send_sem=sems.at[(0,) + at],
            recv_sem=sems.at[(1,) + at],
            device_id=target,
            device_id_type=MESH,
        )

    def start(copies):
        for copy in copies:
            copy.start()

    def finish(copies):
        for copy in copies:
            copy.wait()

    partners = [{"fsdp": a * B + lax.rem(b + bi, B)} for bi in range(1, B)]
    peers = [{"query": lax.rem(q + qi, Q)} for qi in range(1, Q)]
    mine = pl.ds(q * n, n)

    def paired(ref, sems, at=()):
        return [remote(ref, ref, sems, at + (bi + 1,), there) for bi, there in enumerate(partners)]

    def x_rows(first, i):
        return xs.at[pl.ds(pl.multiple_of(first + b * t + i * piece, 16), piece), :]

    x_pair = paired(xs.at[own, :], x_sem)
    kg_pair = [
        remote(
            kgp_ref.at[lax.rem(b + bi, B)], kgs.at[0, mine, own, :], kg_pair_sem, (bi,), partners[bi - 1]
        )
        for bi in range(1, B)
    ]
    kg_peers, kg_extra = (
        [
            remote(kgs.at[g, mine], kgs.at[g, mine], sems, (qi + 1,), there)
            for qi, there in enumerate(peers)
        ]
        for g, sems in ((0, kg_sem), (1, kg_extra_sem))
    )
    kg_end = remote(kgs.at[0, mine], kgs.at[1, mine], kg_end_sem, (), inward)
    x_end = [
        remote(x_rows(0, i), x_rows(extra, i), x_end_sem, (i,), inward) for i in range(CHUNKS)
    ]
    x_extra = [paired(x_rows(extra, i), x_extra_sem, (i,)) for i in range(CHUNKS)]
    pk_pair = paired(pks.at[0, own, :], pk_sem)
    pk_end = remote(pks.at[0, own, :], pks.at[1, own, :], pk_end_sem, (), inward)
    pk_extra = paired(pks.at[1, own, :], pk_extra_sem)

    def w_copy(src, slot, part, send, target):
        return pltpu.make_async_remote_copy(
            src_ref=src,
            dst_ref=wg.at[slot, part],
            send_sem=send.at[slot, part],
            recv_sem=w_recv.at[slot, part],
            device_id=target,
            device_id_type=MESH,
        )

    for part, source in enumerate((wk_hbm, wv_hbm)):

        @pl.when(has_right)
        def _():
            w_copy(source, a, part, w_right, right).start()

        @pl.when(has_left)
        def _():
            w_copy(source, a, part, w_left, left).start()

    kgs[0, mine, own, :] = kgp_ref[b]
    start(kg_pair)

    @pl.when(is_host)
    def _():
        start(x_pair)

    def spread(buffer, sems, axis, me, count):
        copies = []
        for i in range(1, count):
            copy = pltpu.make_async_remote_copy(
                src_ref=buffer.at[me],
                dst_ref=buffer.at[me],
                send_sem=sems.at[0, i],
                recv_sem=sems.at[1, i],
                device_id={axis: lax.rem(me + i, count)},
                device_id_type=MESH,
            )
            copy.start()
            copies.append(copy)
        return copies

    def forward(s):
        before, after = a - s, a + s
        for part in range(2):

            @pl.when(is_host & (before >= 0))
            def _():
                w_copy(wg.at[before, part], before, part, w_left, left).wait_recv()

            @pl.when(is_host & (before >= 0) & has_right)
            def _():
                w_copy(wg.at[before, part], before, part, w_right, right).start()

            @pl.when(is_host & (after < A))
            def _():
                w_copy(wg.at[after, part], after, part, w_right, right).wait_recv()

            @pl.when(is_host & (after < A) & has_left)
            def _():
                w_copy(wg.at[after, part], after, part, w_left, left).start()

    def block(slot):
        weights = jnp.concatenate([wg[slot, 0], wg[slot, 1]], axis=1)
        y = jnp.dot(xs[pl.ds(0, extra), :], weights, preferred_element_type=F32)
        high, low = split(y[B * t : B * t + r] + y[B * t + r :])

        def add(g, value):
            cols = kgs[g, slot]
            prod[g] += value * cols.astype(F32)
            proj[g] += dot_nt(cols, high) + dot_nt(cols, low)

        add(0, y[: B * t])

        @pl.when(has_extra)
        def _():
            add(1, jnp.dot(xs[pl.ds(extra, B * t), :], weights, preferred_element_type=F32))

    def contract(s):
        @pl.when(is_host & (a - s >= 0))
        def _():
            block(a - s)

        @pl.when(is_host & (a + s < A))
        def _():
            block(a + s)

    def pass_rows(first, last):
        for i in range(first, last):

            @pl.when(has_extra)
            def _():
                x_end[i].wait_recv()
                start(x_extra[i])

            @pl.when(is_end)
            def _():
                if i + 1 < CHUNKS:
                    x_end[i].wait_send()
                    x_end[i + 1].start()

    x = x_ref[...]
    xf = x.astype(F32)
    early[q, :, pl.ds(0, r)] = dot_nt(kg_ref[...], pko_ref[...])
    early[q, :, pl.ds(r, r)] = dot_nt(vg_ref[...], pvo_ref[...])
    early[q, :, pl.ds(3 * r, r)] = dot_nt(x, pdo_ref[...])
    early[q, :, pl.ds(4 * r, 2 * r)] = jnp.broadcast_to(
        jnp.sum(xf * xf, axis=1, keepdims=True), (t, 2 * r)
    )
    for load in loads:
        load.wait()
    early[q, :, pl.ds(2 * r, r)] = dot_nt(hid_ref[...], pdi_ref[...])
    early_copies = spread(early, early_sem, "query", q, Q)
    qpg = qpg_ref[...]
    md0 = jnp.sum(xf * gain * qpg.astype(F32), axis=1, keepdims=True) / D
    rg_out = dot_nt(rg_ref[...], pdo_ref[...])
    qpg_out = dot_nt(qpg, xs[pl.ds(B * t, r), :]) + dot_nt(qpg, xs[pl.ds(B * t + r, r), :])
    prod[...] = jnp.zeros_like(prod)
    proj[...] = jnp.zeros_like(proj)

    finish(kg_pair)

    @pl.when(is_host)
    def _():
        start(kg_peers)

    forward(1)

    @pl.when(is_end)
    def _():
        for part in range(2):

            @pl.when(has_right)
            def _():
                w_copy(wg.at[a, part], a, part, w_right, right).wait_send()

            @pl.when(has_left)
            def _():
                w_copy(wg.at[a, part], a, part, w_left, left).wait_send()

        x_end[0].start()
        kg_end.start()

    finish(early_copies)
    whole = early[0]
    for i in range(1, Q):
        whole = whole + early[i]
    place = f // per_seq
    limit = jnp.int32(0)
    for seq in range(seqs):
        limit += jnp.where(place == seq, counts_ref[seq], 0)
    position = lax.rem(f, per_seq) * t + lax.broadcasted_iota(jnp.int32, (t, r), 0)
    mask = jnp.where(position < limit, 1.0, 0.0).astype(F32)
    inv = lax.rsqrt(whole[:, 4 * r :] / D + 1e-05)
    inv_col = inv[:, :1]
    inv_r = inv[:, :r]
    cubed = inv_r * inv_r * inv_r
    back = whole[:, 3 * r : 4 * r] * cubed
    hidden = whole[:, 2 * r : 3 * r] * mask
    pks[0, own, pl.ds(0, r)] = hidden * inv_r
    pks[0, own, pl.ds(r, r)] = whole[:, 3 * r : 4 * r] * (inv_r * inv_r)

    @pl.when(is_host)
    def _():
        start(pk_pair)

    @pl.when(is_end)
    def _():
        pk_end.start()

    @pl.when(has_extra)
    def _():
        kg_end.wait_recv()
        start(kg_extra)

    pass_rows(0, 1)
    normed = (xf * inv_col * gain).astype(BF16)
    attn = dot_nt(normed, pai_ref[...])
    kv_q[q, :, pl.ds(0, r)] = gram(whole[:, :r] * mask, attn)
    kv_q[q, :, pl.ds(r, r)] = gram(whole[:, r : 2 * r] * mask, attn)
    kv_copies = spread(kv_q, kv_q_sem, "query", q, Q)
    pass_rows(1, 2)
    down0 = gram(rg_out + inv_r * qpg_out - back * md0, hidden)

    pass_rows(2, 3)
    for copy in kv_copies:
        copy.wait()
    total = kv_q[0]
    for i in range(1, Q):
        total = total + kv_q[i]
    kv_f[f] = total
    kv_copies = spread(kv_f, kv_f_sem, "fsdp", f, F)
    pass_rows(3, CHUNKS)

    @pl.when(has_extra)
    def _():
        pk_end.wait_recv()
        start(pk_extra)

    forward(2)

    @pl.when(is_end)
    def _():
        x_end[CHUNKS - 1].wait_send()
        kg_end.wait_send()
        pk_end.wait_send()

    @pl.when(is_host)
    def _():
        finish(x_pair)
        finish(kg_peers)
        finish(pk_pair)

    @pl.when(has_extra)
    def _():
        finish(kg_extra)
        for copies in x_extra:
            finish(copies)
        finish(pk_extra)

    @pl.when(is_host)
    def _():
        block(a)

    contract(1)

    def step(s, carry):
        forward(s)
        contract(s - 1)
        return carry

    def by_query(total, at):
        for seq in range(seqs):
            for i in range(r):
                flat[seq, pl.ds(0, 1), pl.ds(at + i * r, r)] = total[seq][i : i + 1, :]

    def score(start, size):
        grads = grads_ref[:, start : start + size]
        parts = []
        for seq in range(seqs):
            row = jnp.broadcast_to(flat[seq, pl.ds(0, 1), pl.ds(start, size)], (16, size))
            high = row.astype(BF16)
            rest = row - high.astype(F32)
            middle = rest.astype(BF16)
            low = (rest - middle.astype(F32)).astype(BF16)
            value = dot_nt(high, grads) + (dot_nt(middle, grads) + dot_nt(low, grads))
            parts.append(value[:1])
        return parts

    def sequences(buffer):
        totals = []
        for seq in range(seqs):
            total = buffer[seq * per_seq]
            for i in range(1, per_seq):
                total = total + buffer[seq * per_seq + i]
            totals.append(total)
        return totals

    lax.fori_loop(3, A - 1, step, 0)
    for copy in kv_copies:
        copy.wait()
    totals = sequences(kv_f)
    by_query([total[:, :r] for total in totals], 0)
    by_query([total[:, r:] for total in totals], r * r)
    scores = score(0, 2 * r * r)
    contract(A - 2)

    d_q[q] = down0

    def add_gram(g):
        dots = jnp.sum(prod[g], axis=1, keepdims=True) / D
        d_q[q] += gram(proj[g] - pks[g, :, pl.ds(r, r)] * dots, pks[g, :, pl.ds(0, r)])

    @pl.when(is_host)
    def _():
        add_gram(0)

    @pl.when(has_extra)
    def _():
        add_gram(1)

    for copy in spread(d_q, d_q_sem, "query", q, Q):
        copy.wait()
    total = d_q[0]
    for i in range(1, Q):
        total = total + d_q[i]
    d_f[f] = total
    d_copies = spread(d_f, d_f_sem, "fsdp", f, F)

    def drain(slot, carry):
        for part in range(2):

            @pl.when((slot <= a) & has_right & is_host)
            def _():
                w_copy(wg.at[slot, part], slot, part, w_right, right).wait_send()

            @pl.when((slot >= a) & has_left & is_host)
            def _():
                w_copy(wg.at[slot, part], slot, part, w_left, left).wait_send()

        return carry

    lax.fori_loop(0, A, drain, 0)
    for copy in d_copies:
        copy.wait()
    by_query(sequences(d_f), 2 * r * r)
    for seq, late_scores in enumerate(score(2 * r * r, r * r)):
        out_ref[pl.ds(seq, 1), :] = scores[seq] + late_scores


def shards(
    F,
    Q,
    resid_in,
    resid_grad,
    query_path_grad,
    hidden_act,
    key_grad,
    value_grad,
    key_weight,
    value_weight,
    norm_gain,
    proj_attn_in,
    proj_key_out,
    proj_value_out,
    proj_down_in,
    proj_down_out,
    query_grads,
    seq_counts,
):
    B = 2
    A = F // B
    t, d = resid_in.shape
    w = key_weight.shape[1]
    r = proj_attn_in.shape[0]
    seqs = seq_counts.shape[0]
    n = key_grad.shape[1] // (w * B)
    vmem = pl.BlockSpec(memory_space=pltpu.VMEM)
    hbm = pl.BlockSpec(memory_space=pl.ANY)
    dma = pltpu.SemaphoreType.DMA
    operands = (
        (resid_in, vmem),
        (resid_grad, hbm),
        (query_path_grad, hbm),
        (hidden_act, hbm),
        (key_grad, vmem),
        (value_grad, vmem),
        (key_weight, hbm),
        (value_weight, hbm),
        (norm_gain.reshape(1, d), vmem),
        (proj_attn_in, vmem),
        (proj_key_out, vmem),
        (proj_value_out, vmem),
        (proj_down_in, hbm),
        (proj_down_out, vmem),
        (query_grads, hbm),
        (seq_counts, pl.BlockSpec(memory_space=pltpu.SMEM)),
    )
    return pl.pallas_call(
        functools.partial(kernel, (F, Q, B, seqs)),
        out_shape=jax.ShapeDtypeStruct((seqs, query_grads.shape[0]), F32),
        in_specs=[spec for _, spec in operands],
        out_specs=vmem,
        scratch_shapes=[
            pltpu.VMEM(resid_grad.shape, BF16),
            pltpu.VMEM(query_path_grad.shape, BF16),
            pltpu.VMEM(hidden_act.shape, BF16),
            pltpu.VMEM(proj_down_in.shape, BF16),
            pltpu.VMEM(query_grads.shape, BF16),
            pltpu.VMEM((A, 2, d, w), BF16),
            pltpu.VMEM((2 * B * t + 2 * r, d), BF16),
            pltpu.VMEM((B, n, t, 2 * w), BF16),
            pltpu.VMEM((2, A, B * t, 2 * w), BF16),
            pltpu.VMEM((Q, t, 6 * r), F32),
            pltpu.VMEM((2, B * t, 2 * r), F32),
            pltpu.VMEM((2, B * t, 2 * w), F32),
            pltpu.VMEM((2, B * t, r), F32),
            pltpu.VMEM((Q, r, 2 * r), F32),
            pltpu.VMEM((F, r, 2 * r), F32),
            pltpu.VMEM((Q, r, r), F32),
            pltpu.VMEM((F, r, r), F32),
            pltpu.VMEM((seqs, 8, 3 * r * r), F32),
            dma((7,)),
            dma((A, 2)),
            dma((A, 2)),
            dma((A, 2)),
            dma((2, B)),
            dma((2, CHUNKS)),
            dma((2, CHUNKS, B)),
            dma((2, B)),
            dma((2, Q)),
            dma((2,)),
            dma((2, Q)),
            dma((2, Q)),
            dma((2, B)),
            dma((2,)),
            dma((2, B)),
            dma((2, Q)),
            dma((2, F)),
            dma((2, Q)),
            dma((2, F)),
        ],
        compiler_params=pltpu.CompilerParams(
            collective_id=0, has_side_effects=True, vmem_limit_bytes=56 * 2**20
        ),
    )(*(operand for operand, _ in operands))


def solution(mesh):
    placed = (
        P(("parts", "fsdp"), "query"),
        P(("parts", "fsdp"), "query"),
        P(("parts", "fsdp"), "query"),
        P(("parts", "fsdp"), "query"),
        P(("parts", "fsdp"), "query"),
        P(("parts", "fsdp"), "query"),
        P("query", "fsdp"),
        P("query", "fsdp"),
        P("query"),
        P(None, "query"),
        P(None, "query"),
        P(None, "query"),
        P(None, "query"),
        P(None, "query"),
        P(("fsdp", "query"), None),
        P("parts"),
    )
    return jax.shard_map(
        functools.partial(shards, mesh.shape["fsdp"], mesh.shape["query"]),
        mesh=mesh,
        in_specs=placed,
        out_specs=P("parts", ("fsdp", "query")),
        check_vma=False,
    )
```

```python
import functools

import jax
import jax.numpy as jnp
from jax import lax
from jax.experimental import pallas as pl
from jax.experimental.pallas import tpu as pltpu
from jax.sharding import PartitionSpec as P

D = 8192
LEN = 2048
CHUNKS = 4
MESH = pl.DeviceIdType.MESH
F32 = jnp.float32
BF16 = jnp.bfloat16


def dot_nt(left, right):
    return lax.dot_general(left, right, (((1,), (1,)), ((), ())), preferred_element_type=F32)


def gram(left, right):
    return lax.dot_general(
        left,
        right,
        (((0,), (0,)), ((), ())),
        precision=lax.Precision.HIGHEST,
        preferred_element_type=F32,
    )


def split(value):
    high = value.astype(BF16)
    return high, (value - high.astype(F32)).astype(BF16)


def kernel(
    sizes,
    x_ref,
    rg_hbm,
    qpg_hbm,
    hid_hbm,
    kg_ref,
    vg_ref,
    wk_hbm,
    wv_hbm,
    gain_ref,
    pai_ref,
    pko_ref,
    pvo_ref,
    pdi_hbm,
    pdo_ref,
    grads_hbm,
    counts_ref,
    out_ref,
    rg_ref,
    qpg_ref,
    hid_ref,
    pdi_ref,
    grads_ref,
    wg,
    xs,
    kgp_ref,
    kgs,
    early,
    squares,
    pks,
    prod,
    proj,
    kv_q,
    kv_f,
    d_q,
    d_f,
    flat,
    load_sem,
    w_recv,
    w_right,
    w_left,
    x_sem,
    x_end_sem,
    x_extra_sem,
    kg_pair_sem,
    kg_sem,
    kg_end_sem,
    kg_extra_sem,
    early_sem,
    squares_sem,
    pk_sem,
    pk_end_sem,
    pk_extra_sem,
    kv_q_sem,
    kv_f_sem,
    d_q_sem,
    d_f_sem,
):
    F, Q, B, seqs = sizes
    A = F // B
    per_seq = F // seqs
    n = kgp_ref.shape[1]
    t, d = x_ref.shape
    w = wk_hbm.shape[1]
    r = pdo_ref.shape[0]
    f, q = lax.axis_index("fsdp"), lax.axis_index("query")
    a, b = f // B, lax.rem(f, B)

    barrier = pltpu.get_barrier_semaphore()
    others = 0
    for i in range(1, F):
        pl.semaphore_signal(
            barrier, inc=1, device_id={"fsdp": lax.rem(f + i, F)}, device_id_type=MESH
        )
        others += 1
    for qi in range(1, Q):
        pl.semaphore_signal(
            barrier, inc=1, device_id={"query": lax.rem(q + qi, Q)}, device_id_type=MESH
        )
        others += 1

    loads = [
        pltpu.make_async_copy(src, dst, load_sem.at[i])
        for i, (src, dst) in enumerate(
            (
                (hid_hbm, hid_ref),
                (pdi_hbm, pdi_ref),
                (qpg_hbm, qpg_ref),
                (rg_hbm, rg_ref),
                (wk_hbm, wg.at[a, 0]),
                (wv_hbm, wg.at[a, 1]),
                (grads_hbm, grads_ref),
            )
        )
    ]
    for load in loads:
        load.start()
    gain = gain_ref[...].astype(F32)
    own = pl.ds(pl.multiple_of(b * t, t), t)
    xs[own, :] = (x_ref[...].astype(F32) * gain).astype(BF16)
    gp_high, gp_low = split(pdo_ref[...].astype(F32) * gain)
    xs[pl.ds(B * t, r), :] = gp_high
    xs[pl.ds(B * t + r, r), :] = gp_low
    for bi in range(B):
        for i in range(n):
            at = (i * B + bi) * w
            kgp_ref[bi, i, :, pl.ds(0, w)] = kg_ref[:, at : at + w]
            kgp_ref[bi, i, :, pl.ds(w, w)] = vg_ref[:, at : at + w]
    pl.semaphore_wait(barrier, others)

    right = {"fsdp": jnp.minimum(f + B, F - 1 - lax.rem(F - 1 - f, B))}
    left = {"fsdp": jnp.maximum(f - B, b)}
    is_end = (a == 0) | (a == A - 1)
    is_host = (a > 0) & (a < A - 1)
    has_extra = (a == 1) | (a == A - 2)
    inward = {"fsdp": jnp.where(a == 0, f + B, f - B)}
    has_right, has_left = a < A - 2, a > 1
    extra = B * t + 2 * r
    piece = t // CHUNKS

    def remote(src, dst, sems, at, target):
        return pltpu.make_async_remote_copy(
            src_ref=src,
            dst_ref=dst,
            send_sem=sems.at[(0,) + at],
            recv_sem=sems.at[(1,) + at],
            device_id=target,
            device_id_type=MESH,
        )

    def start(copies):
        for copy in copies:
            copy.start()

    def finish(copies):
        for copy in copies:
            copy.wait()

    partners = [{"fsdp": a * B + lax.rem(b + bi, B)} for bi in range(1, B)]
    peers = [{"query": lax.rem(q + qi, Q)} for qi in range(1, Q)]
    mine = pl.ds(q * n, n)

    def paired(ref, sems, at=()):
        return [remote(ref, ref, sems, at + (bi + 1,), there) for bi, there in enumerate(partners)]

    def x_rows(first, i):
        return xs.at[pl.ds(pl.multiple_of(first + b * t + i * piece, 16), piece), :]

    x_pair = paired(xs.at[own, :], x_sem)
    kg_pair = [
        remote(
            kgp_ref.at[lax.rem(b + bi, B)], kgs.at[0, mine, own, :], kg_pair_sem, (bi,), partners[bi - 1]
        )
        for bi in range(1, B)
    ]
    kg_peers, kg_extra = (
        [
            remote(kgs.at[g, mine], kgs.at[g, mine], sems, (qi + 1,), there)
            for qi, there in enumerate(peers)
        ]
        for g, sems in ((0, kg_sem), (1, kg_extra_sem))
    )
    kg_end = remote(kgs.at[0, mine], kgs.at[1, mine], kg_end_sem, (), inward)
    x_end = [
        remote(x_rows(0, i), x_rows(extra, i), x_end_sem, (i,), inward) for i in range(CHUNKS)
    ]
    x_extra = [paired(x_rows(extra, i), x_extra_sem, (i,)) for i in range(CHUNKS)]
    pk_pair = paired(pks.at[0, own, :], pk_sem)
    pk_end = remote(pks.at[0, own, :], pks.at[1, own, :], pk_end_sem, (), inward)
    pk_extra = paired(pks.at[1, own, :], pk_extra_sem)

    def w_copy(src, slot, part, send, target):
        return pltpu.make_async_remote_copy(
            src_ref=src,
            dst_ref=wg.at[slot, part],
            send_sem=send.at[slot, part],
            recv_sem=w_recv.at[slot, part],
            device_id=target,
            device_id_type=MESH,
        )

    for part, source in enumerate((wk_hbm, wv_hbm)):

        @pl.when(has_right)
        def _():
            w_copy(source, a, part, w_right, right).start()

        @pl.when(has_left)
        def _():
            w_copy(source, a, part, w_left, left).start()

    kgs[0, mine, own, :] = kgp_ref[b]
    start(kg_pair)

    @pl.when(is_host)
    def _():
        start(x_pair)

    def spread(buffer, sems, axis, me, count):
        copies = []
        for i in range(1, count):
            copy = pltpu.make_async_remote_copy(
                src_ref=buffer.at[me],
                dst_ref=buffer.at[me],
                send_sem=sems.at[0, i],
                recv_sem=sems.at[1, i],
                device_id={axis: lax.rem(me + i, count)},
                device_id_type=MESH,
            )
            copy.start()
            copies.append(copy)
        return copies

    def forward(s):
        before, after = a - s, a + s
        for part in range(2):

            @pl.when(is_host & (before >= 0))
            def _():
                w_copy(wg.at[before, part], before, part, w_left, left).wait_recv()

            @pl.when(is_host & (before >= 0) & has_right)
            def _():
                w_copy(wg.at[before, part], before, part, w_right, right).start()

            @pl.when(is_host & (after < A))
            def _():
                w_copy(wg.at[after, part], after, part, w_right, right).wait_recv()

            @pl.when(is_host & (after < A) & has_left)
            def _():
                w_copy(wg.at[after, part], after, part, w_left, left).start()

    def block(g, slot):
        weights = jnp.concatenate([wg[slot, 0], wg[slot, 1]], axis=1)
        rows = xs[pl.ds(g * B * t, extra), :]
        y = jnp.dot(rows, weights, preferred_element_type=F32)
        gains = y[B * t :] if g == 0 else y[: 2 * r]
        tokens = y[: B * t] if g == 0 else y[2 * r :]
        high, low = split(gains[:r] + gains[r:])
        cols = kgs[g, slot]
        prod[g] += tokens * cols.astype(F32)
        proj[g] += dot_nt(cols, high) + dot_nt(cols, low)

    def contract(s):
        @pl.when(is_host & (a - s >= 0))
        def _():
            block(0, a - s)

        @pl.when(is_host & (a + s < A))
        def _():
            block(0, a + s)

    def pass_rows(i):
        @pl.when(has_extra)
        def _():
            x_end[i].wait_recv()
            start(x_extra[i])

    x = x_ref[...]
    xf = x.astype(F32)
    early[q, :, pl.ds(0, r)] = dot_nt(kg_ref[...], pko_ref[...])
    early[q, :, pl.ds(r, r)] = dot_nt(vg_ref[...], pvo_ref[...])
    early[q, :, pl.ds(3 * r, r)] = dot_nt(x, pdo_ref[...])
    total = jnp.broadcast_to(jnp.sum(xf * xf, axis=1, keepdims=True), (t, 2 * r))
    squares[q] = jnp.transpose(total)[:8]
    early_copies = spread(squares, squares_sem, "query", q, Q)
    for load in loads:
        load.wait()
    early[q, :, pl.ds(2 * r, r)] = dot_nt(hid_ref[...], pdi_ref[...])
    early_copies += spread(early, early_sem, "query", q, Q)
    qpg = qpg_ref[...]
    md0 = jnp.sum(xf * gain * qpg.astype(F32), axis=1, keepdims=True) / D
    rg_out = dot_nt(rg_ref[...], pdo_ref[...])
    qpg_out = dot_nt(qpg, xs[pl.ds(B * t, r), :]) + dot_nt(qpg, xs[pl.ds(B * t + r, r), :])
    prod[...] = jnp.zeros_like(prod)
    proj[...] = jnp.zeros_like(proj)

    finish(kg_pair)

    @pl.when(is_host)
    def _():
        start(kg_peers)

    @pl.when(is_end)
    def _():
        kg_end.start()
        start(x_end)

    finish(early_copies)
    whole = early[0]
    for i in range(1, Q):
        whole = whole + early[i]
    place = f // per_seq
    limit = jnp.int32(0)
    for seq in range(seqs):
        limit += jnp.where(place == seq, counts_ref[seq], 0)
    position = lax.rem(f, per_seq) * t + lax.broadcasted_iota(jnp.int32, (t, r), 0)
    mask = jnp.where(position < limit, 1.0, 0.0).astype(F32)
    total = squares[0]
    for i in range(1, Q):
        total = total + squares[i]
    total = jnp.transpose(jnp.broadcast_to(total[:1], (2 * r, t)))
    inv = lax.rsqrt(total / D + 1e-05)
    inv_col = inv[:, :1]
    inv_r = inv[:, :r]
    cubed = inv_r * inv_r * inv_r
    back = whole[:, 3 * r : 4 * r] * cubed
    hidden = whole[:, 2 * r : 3 * r] * mask
    pks[0, own, pl.ds(0, r)] = hidden * inv_r
    pks[0, own, pl.ds(r, r)] = whole[:, 3 * r : 4 * r] * (inv_r * inv_r)

    @pl.when(is_host)
    def _():
        start(pk_pair)

    @pl.when(is_end)
    def _():
        pk_end.start()

    forward(1)

    @pl.when(has_extra)
    def _():
        kg_end.wait_recv()
        start(kg_extra)

    normed = (xf * inv_col * gain).astype(BF16)
    attn = dot_nt(normed, pai_ref[...])
    kv_q[q, :, pl.ds(0, r)] = gram(whole[:, :r] * mask, attn)
    kv_q[q, :, pl.ds(r, r)] = gram(whole[:, r : 2 * r] * mask, attn)
    kv_copies = spread(kv_q, kv_q_sem, "query", q, Q)
    pass_rows(0)
    down0 = gram(rg_out + inv_r * qpg_out - back * md0, hidden)

    pass_rows(1)
    for copy in kv_copies:
        copy.wait()
    total = kv_q[0]
    for i in range(1, Q):
        total = total + kv_q[i]
    kv_f[f] = total
    kv_copies = spread(kv_f, kv_f_sem, "fsdp", f, F)
    @pl.when(is_host)
    def _():
        finish(x_pair)
        finish(kg_peers)
        block(0, a)

    contract(1)
    pass_rows(2)
    forward(2)
    for i in range(3, CHUNKS):
        pass_rows(i)

    @pl.when(has_extra)
    def _():
        pk_end.wait_recv()
        start(pk_extra)

    def step(s, carry):
        forward(s)
        contract(s - 1)
        return carry

    def by_query(total, at):
        for seq in range(seqs):
            for i in range(r):
                flat[seq, pl.ds(0, 1), pl.ds(at + i * r, r)] = total[seq][i : i + 1, :]

    def score(start, size):
        grads = grads_ref[:, start : start + size]
        parts = []
        for seq in range(seqs):
            row = jnp.broadcast_to(flat[seq, pl.ds(0, 1), pl.ds(start, size)], (16, size))
            high = row.astype(BF16)
            rest = row - high.astype(F32)
            middle = rest.astype(BF16)
            low = (rest - middle.astype(F32)).astype(BF16)
            value = dot_nt(high, grads) + (dot_nt(middle, grads) + dot_nt(low, grads))
            parts.append(value[:1])
        return parts

    def sequences(buffer):
        totals = []
        for seq in range(seqs):
            total = buffer[seq * per_seq]
            for i in range(1, per_seq):
                total = total + buffer[seq * per_seq + i]
            totals.append(total)
        return totals

    lax.fori_loop(3, A - 1, step, 0)
    contract(A - 2)

    @pl.when(is_host)
    def _():
        finish(pk_pair)

    def extra_block(slot, carry):
        block(1, slot)
        return carry

    @pl.when(has_extra)
    def _():
        finish(kg_extra)
        for copies in x_extra:
            finish(copies)
        lax.fori_loop(0, A, extra_block, 0)
        finish(pk_extra)

    d_q[q] = down0

    def add_gram(g):
        dots = jnp.sum(prod[g], axis=1, keepdims=True) / D
        d_q[q] += gram(proj[g] - pks[g, :, pl.ds(r, r)] * dots, pks[g, :, pl.ds(0, r)])

    @pl.when(is_host)
    def _():
        add_gram(0)

    @pl.when(has_extra)
    def _():
        add_gram(1)

    for copy in spread(d_q, d_q_sem, "query", q, Q):
        copy.wait()
    total = d_q[0]
    for i in range(1, Q):
        total = total + d_q[i]
    d_f[f] = total
    d_copies = spread(d_f, d_f_sem, "fsdp", f, F)

    def drain(slot, carry):
        for part in range(2):

            @pl.when((slot <= a) & has_right & (is_host | (slot == a)))
            def _():
                w_copy(wg.at[slot, part], slot, part, w_right, right).wait_send()

            @pl.when((slot >= a) & has_left & (is_host | (slot == a)))
            def _():
                w_copy(wg.at[slot, part], slot, part, w_left, left).wait_send()

        return carry

    lax.fori_loop(0, A, drain, 0)

    @pl.when(is_end)
    def _():
        for copy in [kg_end, pk_end] + x_end:
            copy.wait_send()

    for copy in kv_copies:
        copy.wait()
    totals = sequences(kv_f)
    by_query([total[:, :r] for total in totals], 0)
    by_query([total[:, r:] for total in totals], r * r)
    scores = score(0, 2 * r * r)
    for copy in d_copies:
        copy.wait()
    by_query(sequences(d_f), 2 * r * r)
    for seq, late_scores in enumerate(score(2 * r * r, r * r)):
        out_ref[pl.ds(seq, 1), :] = scores[seq] + late_scores


def shards(
    F,
    Q,
    resid_in,
    resid_grad,
    query_path_grad,
    hidden_act,
    key_grad,
    value_grad,
    key_weight,
    value_weight,
    norm_gain,
    proj_attn_in,
    proj_key_out,
    proj_value_out,
    proj_down_in,
    proj_down_out,
    query_grads,
    seq_counts,
):
    B = 2
    A = F // B
    t, d = resid_in.shape
    w = key_weight.shape[1]
    r = proj_attn_in.shape[0]
    seqs = seq_counts.shape[0]
    n = key_grad.shape[1] // (w * B)
    vmem = pl.BlockSpec(memory_space=pltpu.VMEM)
    hbm = pl.BlockSpec(memory_space=pl.ANY)
    dma = pltpu.SemaphoreType.DMA
    operands = (
        (resid_in, vmem),
        (resid_grad, hbm),
        (query_path_grad, hbm),
        (hidden_act, hbm),
        (key_grad, vmem),
        (value_grad, vmem),
        (key_weight, hbm),
        (value_weight, hbm),
        (norm_gain.reshape(1, d), vmem),
        (proj_attn_in, vmem),
        (proj_key_out, vmem),
        (proj_value_out, vmem),
        (proj_down_in, hbm),
        (proj_down_out, vmem),
        (query_grads, hbm),
        (seq_counts, pl.BlockSpec(memory_space=pltpu.SMEM)),
    )
    return pl.pallas_call(
        functools.partial(kernel, (F, Q, B, seqs)),
        out_shape=jax.ShapeDtypeStruct((seqs, query_grads.shape[0]), F32),
        in_specs=[spec for _, spec in operands],
        out_specs=vmem,
        scratch_shapes=[
            pltpu.VMEM(resid_grad.shape, BF16),
            pltpu.VMEM(query_path_grad.shape, BF16),
            pltpu.VMEM(hidden_act.shape, BF16),
            pltpu.VMEM(proj_down_in.shape, BF16),
            pltpu.VMEM(query_grads.shape, BF16),
            pltpu.VMEM((A, 2, d, w), BF16),
            pltpu.VMEM((2 * B * t + 2 * r, d), BF16),
            pltpu.VMEM((B, n, t, 2 * w), BF16),
            pltpu.VMEM((2, A, B * t, 2 * w), BF16),
            pltpu.VMEM((Q, t, 4 * r), F32),
            pltpu.VMEM((Q, 8, t), F32),
            pltpu.VMEM((2, B * t, 2 * r), F32),
            pltpu.VMEM((2, B * t, 2 * w), F32),
            pltpu.VMEM((2, B * t, r), F32),
            pltpu.VMEM((Q, r, 2 * r), F32),
            pltpu.VMEM((F, r, 2 * r), F32),
            pltpu.VMEM((Q, r, r), F32),
            pltpu.VMEM((F, r, r), F32),
            pltpu.VMEM((seqs, 8, 3 * r * r), F32),
            dma((7,)),
            dma((A, 2)),
            dma((A, 2)),
            dma((A, 2)),
            dma((2, B)),
            dma((2, CHUNKS)),
            dma((2, CHUNKS, B)),
            dma((2, B)),
            dma((2, Q)),
            dma((2,)),
            dma((2, Q)),
            dma((2, Q)),
            dma((2, Q)),
            dma((2, B)),
            dma((2,)),
            dma((2, B)),
            dma((2, Q)),
            dma((2, F)),
            dma((2, Q)),
            dma((2, F)),
        ],
        compiler_params=pltpu.CompilerParams(
            collective_id=0, has_side_effects=True, vmem_limit_bytes=56 * 2**20
        ),
    )(*(operand for operand, _ in operands))


def solution(mesh):
    placed = (
        P(("parts", "fsdp"), "query"),
        P(("parts", "fsdp"), "query"),
        P(("parts", "fsdp"), "query"),
        P(("parts", "fsdp"), "query"),
        P(("parts", "fsdp"), "query"),
        P(("parts", "fsdp"), "query"),
        P("query", "fsdp"),
        P("query", "fsdp"),
        P("query"),
        P(None, "query"),
        P(None, "query"),
        P(None, "query"),
        P(None, "query"),
        P(None, "query"),
        P(("fsdp", "query"), None),
        P("parts"),
    )
    return jax.shard_map(
        functools.partial(shards, mesh.shape["fsdp"], mesh.shape["query"]),
        mesh=mesh,
        in_specs=placed,
        out_specs=P("parts", ("fsdp", "query")),
        check_vma=False,
    )
```

```python
import functools

import jax
import jax.numpy as jnp
from jax import lax
from jax.experimental import pallas as pl
from jax.experimental.pallas import tpu as pltpu
from jax.sharding import PartitionSpec as P

D = 8192
LEN = 2048
CHUNKS = 8
MESH = pl.DeviceIdType.MESH
F32 = jnp.float32
BF16 = jnp.bfloat16


def dot_nt(left, right):
    return lax.dot_general(left, right, (((1,), (1,)), ((), ())), preferred_element_type=F32)


def gram(left, right):
    return lax.dot_general(
        left,
        right,
        (((0,), (0,)), ((), ())),
        precision=lax.Precision.HIGHEST,
        preferred_element_type=F32,
    )


def split(value):
    high = value.astype(BF16)
    return high, (value - high.astype(F32)).astype(BF16)


def kernel(
    sizes,
    x_ref,
    rg_hbm,
    qpg_hbm,
    hid_hbm,
    kg_ref,
    vg_ref,
    wk_hbm,
    wv_hbm,
    gain_ref,
    pai_ref,
    pko_ref,
    pvo_ref,
    pdi_hbm,
    pdo_ref,
    grads_hbm,
    counts_ref,
    out_ref,
    rg_ref,
    qpg_ref,
    hid_ref,
    pdi_ref,
    grads_ref,
    wg,
    xs,
    kgp_ref,
    kgs,
    early,
    squares,
    pks,
    prod,
    proj,
    kv_q,
    kv_f,
    d_q,
    d_f,
    flat,
    load_sem,
    w_recv,
    w_right,
    w_left,
    x_sem,
    x_end_sem,
    x_extra_sem,
    kg_pair_sem,
    kg_sem,
    kg_end_sem,
    kg_extra_sem,
    early_sem,
    squares_sem,
    pk_sem,
    pk_end_sem,
    pk_extra_sem,
    kv_q_sem,
    kv_f_sem,
    d_q_sem,
    d_f_sem,
):
    F, Q, B, seqs = sizes
    A = F // B
    per_seq = F // seqs
    n = kgp_ref.shape[1]
    t, d = x_ref.shape
    w = wk_hbm.shape[1]
    r = pdo_ref.shape[0]
    f, q = lax.axis_index("fsdp"), lax.axis_index("query")
    a, b = f // B, lax.rem(f, B)

    barrier = pltpu.get_barrier_semaphore()
    others = 0
    for i in range(1, F):
        pl.semaphore_signal(
            barrier, inc=1, device_id={"fsdp": lax.rem(f + i, F)}, device_id_type=MESH
        )
        others += 1
    for qi in range(1, Q):
        pl.semaphore_signal(
            barrier, inc=1, device_id={"query": lax.rem(q + qi, Q)}, device_id_type=MESH
        )
        others += 1

    loads = [
        pltpu.make_async_copy(src, dst, load_sem.at[i])
        for i, (src, dst) in enumerate(
            (
                (hid_hbm, hid_ref),
                (pdi_hbm, pdi_ref),
                (qpg_hbm, qpg_ref),
                (rg_hbm, rg_ref),
                (wk_hbm, wg.at[a, 0]),
                (wv_hbm, wg.at[a, 1]),
                (grads_hbm, grads_ref),
            )
        )
    ]
    for load in loads:
        load.start()
    gain = gain_ref[...].astype(F32).reshape(1, d)
    own = pl.ds(pl.multiple_of(b * t, t), t)
    xs[own, :] = (x_ref[...].astype(F32) * gain).astype(BF16)
    gp_high, gp_low = split(pdo_ref[...].astype(F32) * gain)
    xs[pl.ds(B * t, r), :] = gp_high
    xs[pl.ds(B * t + r, r), :] = gp_low
    for bi in range(B):
        for i in range(n):
            at = (i * B + bi) * w
            kgp_ref[bi, i, :, pl.ds(0, w)] = kg_ref[:, at : at + w]
            kgp_ref[bi, i, :, pl.ds(w, w)] = vg_ref[:, at : at + w]
    pl.semaphore_wait(barrier, others)

    right = {"fsdp": jnp.minimum(f + B, F - 1 - lax.rem(F - 1 - f, B))}
    left = {"fsdp": jnp.maximum(f - B, b)}
    is_end = (a == 0) | (a == A - 1)
    is_host = (a > 0) & (a < A - 1)
    has_extra = (a == 1) | (a == A - 2)
    inward = {"fsdp": jnp.where(a == 0, f + B, f - B)}
    has_right, has_left = a < A - 2, a > 1
    extra = B * t + 2 * r
    piece = t // CHUNKS

    def remote(src, dst, sems, at, target):
        return pltpu.make_async_remote_copy(
            src_ref=src,
            dst_ref=dst,
            send_sem=sems.at[(0,) + at],
            recv_sem=sems.at[(1,) + at],
            device_id=target,
            device_id_type=MESH,
        )

    def start(copies):
        for copy in copies:
            copy.start()

    def finish(copies):
        for copy in copies:
            copy.wait()

    partners = [{"fsdp": a * B + lax.rem(b + bi, B)} for bi in range(1, B)]
    peers = [{"query": lax.rem(q + qi, Q)} for qi in range(1, Q)]
    mine = pl.ds(q * n, n)

    def paired(ref, sems, at=()):
        return [remote(ref, ref, sems, at + (bi + 1,), there) for bi, there in enumerate(partners)]

    def x_rows(first, i):
        return xs.at[pl.ds(pl.multiple_of(first + b * t + i * piece, 16), piece), :]

    x_pair = paired(xs.at[own, :], x_sem)
    kg_pair = [
        remote(
            kgp_ref.at[lax.rem(b + bi, B)], kgs.at[0, mine, own, :], kg_pair_sem, (bi,), partners[bi - 1]
        )
        for bi in range(1, B)
    ]
    kg_peers, kg_extra = (
        [
            remote(kgs.at[g, mine], kgs.at[g, mine], sems, (qi + 1,), there)
            for qi, there in enumerate(peers)
        ]
        for g, sems in ((0, kg_sem), (1, kg_extra_sem))
    )
    kg_end = remote(kgs.at[0, mine], kgs.at[1, mine], kg_end_sem, (), inward)
    x_end = [
        remote(x_rows(0, i), x_rows(extra, i), x_end_sem, (i,), inward) for i in range(CHUNKS)
    ]
    x_extra = [paired(x_rows(extra, i), x_extra_sem, (i,)) for i in range(CHUNKS)]
    pk_pair = paired(pks.at[0, own, :], pk_sem)
    pk_end = remote(pks.at[0, own, :], pks.at[1, own, :], pk_end_sem, (), inward)
    pk_extra = paired(pks.at[1, own, :], pk_extra_sem)

    def w_copy(src, slot, part, send, target):
        return pltpu.make_async_remote_copy(
            src_ref=src,
            dst_ref=wg.at[slot, part],
            send_sem=send.at[slot, part],
            recv_sem=w_recv.at[slot, part],
            device_id=target,
            device_id_type=MESH,
        )

    for part, source in enumerate((wk_hbm, wv_hbm)):

        @pl.when(has_right)
        def _():
            w_copy(source, a, part, w_right, right).start()

        @pl.when(has_left)
        def _():
            w_copy(source, a, part, w_left, left).start()

    kgs[0, mine, own, :] = kgp_ref[b]
    start(kg_pair)

    @pl.when(is_host)
    def _():
        start(x_pair)

    def spread(buffer, sems, axis, me, count):
        copies = []
        for i in range(1, count):
            copy = pltpu.make_async_remote_copy(
                src_ref=buffer.at[me],
                dst_ref=buffer.at[me],
                send_sem=sems.at[0, i],
                recv_sem=sems.at[1, i],
                device_id={axis: lax.rem(me + i, count)},
                device_id_type=MESH,
            )
            copy.start()
            copies.append(copy)
        return copies

    def forward(s):
        before, after = a - s, a + s
        for part in range(2):

            @pl.when(is_host & (before >= 0))
            def _():
                w_copy(wg.at[before, part], before, part, w_left, left).wait_recv()

            @pl.when(is_host & (before >= 0) & has_right)
            def _():
                w_copy(wg.at[before, part], before, part, w_right, right).start()

            @pl.when(is_host & (after < A))
            def _():
                w_copy(wg.at[after, part], after, part, w_right, right).wait_recv()

            @pl.when(is_host & (after < A) & has_left)
            def _():
                w_copy(wg.at[after, part], after, part, w_left, left).start()

    def block(g, slot):
        weights = jnp.concatenate([wg[slot, 0], wg[slot, 1]], axis=1)
        rows = xs[pl.ds(g * B * t, extra), :]
        y = jnp.dot(rows, weights, preferred_element_type=F32)
        gains = y[B * t :] if g == 0 else y[: 2 * r]
        tokens = y[: B * t] if g == 0 else y[2 * r :]
        high, low = split(gains[:r] + gains[r:])
        cols = kgs[g, slot]
        prod[g] += tokens * cols.astype(F32)
        proj[g] += dot_nt(cols, high) + dot_nt(cols, low)

    def contract(s):
        @pl.when(is_host & (a - s >= 0))
        def _():
            block(0, a - s)

        @pl.when(is_host & (a + s < A))
        def _():
            block(0, a + s)

    def pass_rows(i):
        @pl.when(has_extra)
        def _():
            x_end[i].wait_recv()
            start(x_extra[i])

    x = x_ref[...]
    xf = x.astype(F32)
    early[q, :, pl.ds(0, r)] = dot_nt(kg_ref[...], pko_ref[...])
    early[q, :, pl.ds(r, r)] = dot_nt(vg_ref[...], pvo_ref[...])
    early[q, :, pl.ds(3 * r, r)] = dot_nt(x, pdo_ref[...])
    total = jnp.broadcast_to(jnp.sum(xf * xf, axis=1, keepdims=True), (t, 2 * r))
    squares[q] = jnp.transpose(total)[:8]
    early_copies = spread(squares, squares_sem, "query", q, Q)
    for load in loads:
        load.wait()
    early[q, :, pl.ds(2 * r, r)] = dot_nt(hid_ref[...], pdi_ref[...])
    early_copies += spread(early, early_sem, "query", q, Q)
    qpg = qpg_ref[...]
    md0 = jnp.sum(xf * gain * qpg.astype(F32), axis=1, keepdims=True) / D
    rg_out = dot_nt(rg_ref[...], pdo_ref[...])
    qpg_out = dot_nt(qpg, xs[pl.ds(B * t, r), :]) + dot_nt(qpg, xs[pl.ds(B * t + r, r), :])
    prod[...] = jnp.zeros_like(prod)
    proj[...] = jnp.zeros_like(proj)

    finish(kg_pair)

    @pl.when(is_host)
    def _():
        start(kg_peers)

    @pl.when(is_end)
    def _():
        kg_end.start()
        start(x_end)

    finish(early_copies)
    whole = early[0]
    for i in range(1, Q):
        whole = whole + early[i]
    place = f // per_seq
    limit = jnp.int32(0)
    for seq in range(seqs):
        limit += jnp.where(place == seq, counts_ref[seq], 0)
    position = lax.rem(f, per_seq) * t + lax.broadcasted_iota(jnp.int32, (t, r), 0)
    mask = jnp.where(position < limit, 1.0, 0.0).astype(F32)
    total = squares[0]
    for i in range(1, Q):
        total = total + squares[i]
    total = jnp.transpose(jnp.broadcast_to(total[:1], (2 * r, t)))
    inv = lax.rsqrt(total / D + 1e-05)
    inv_col = inv[:, :1]
    inv_r = inv[:, :r]
    cubed = inv_r * inv_r * inv_r
    back = whole[:, 3 * r : 4 * r] * cubed
    hidden = whole[:, 2 * r : 3 * r] * mask
    pks[0, own, pl.ds(0, r)] = hidden * inv_r
    pks[0, own, pl.ds(r, r)] = whole[:, 3 * r : 4 * r] * (inv_r * inv_r)

    @pl.when(is_host)
    def _():
        start(pk_pair)

    @pl.when(is_end)
    def _():
        pk_end.start()

    forward(1)

    @pl.when(has_extra)
    def _():
        kg_end.wait_recv()
        start(kg_extra)

    normed = (xf * inv_col * gain).astype(BF16)
    attn = dot_nt(normed, pai_ref[...])
    kv_q[q, :, pl.ds(0, r)] = gram(whole[:, :r] * mask, attn)
    kv_q[q, :, pl.ds(r, r)] = gram(whole[:, r : 2 * r] * mask, attn)
    kv_copies = spread(kv_q, kv_q_sem, "query", q, Q)
    for i in range(2):
        pass_rows(i)
    down0 = gram(rg_out + inv_r * qpg_out - back * md0, hidden)

    for i in range(2, 4):
        pass_rows(i)
    for copy in kv_copies:
        copy.wait()
    total = kv_q[0]
    for i in range(1, Q):
        total = total + kv_q[i]
    kv_f[f] = total
    kv_copies = spread(kv_f, kv_f_sem, "fsdp", f, F)
    pass_rows(4)

    @pl.when(is_host)
    def _():
        finish(x_pair)
        finish(kg_peers)
        block(0, a)

    contract(1)
    for i in range(5, CHUNKS):
        pass_rows(i)
    forward(2)

    @pl.when(has_extra)
    def _():
        pk_end.wait_recv()
        start(pk_extra)

    def step(s, carry):
        forward(s)
        contract(s - 1)
        return carry

    def by_query(total, at):
        for seq in range(seqs):
            for i in range(r):
                flat[seq, pl.ds(0, 1), pl.ds(at + i * r, r)] = total[seq][i : i + 1, :]

    def score(start, size):
        grads = grads_ref[:, start : start + size]
        parts = []
        for seq in range(seqs):
            row = jnp.broadcast_to(flat[seq, pl.ds(0, 1), pl.ds(start, size)], (16, size))
            high = row.astype(BF16)
            rest = row - high.astype(F32)
            middle = rest.astype(BF16)
            low = (rest - middle.astype(F32)).astype(BF16)
            value = dot_nt(high, grads) + (dot_nt(middle, grads) + dot_nt(low, grads))
            parts.append(value[:1])
        return parts

    def sequences(buffer):
        totals = []
        for seq in range(seqs):
            total = buffer[seq * per_seq]
            for i in range(1, per_seq):
                total = total + buffer[seq * per_seq + i]
            totals.append(total)
        return totals

    lax.fori_loop(3, A - 1, step, 0)
    contract(A - 2)

    @pl.when(is_host)
    def _():
        finish(pk_pair)

    def extra_block(slot, carry):
        block(1, slot)
        return carry

    @pl.when(has_extra)
    def _():
        finish(kg_extra)
        for copies in x_extra:
            finish(copies)
        lax.fori_loop(0, A, extra_block, 0)
        finish(pk_extra)

    d_q[q] = down0

    def add_gram(g):
        dots = jnp.sum(prod[g], axis=1, keepdims=True) / D
        d_q[q] += gram(proj[g] - pks[g, :, pl.ds(r, r)] * dots, pks[g, :, pl.ds(0, r)])

    @pl.when(is_host)
    def _():
        add_gram(0)

    @pl.when(has_extra)
    def _():
        add_gram(1)

    for copy in spread(d_q, d_q_sem, "query", q, Q):
        copy.wait()
    total = d_q[0]
    for i in range(1, Q):
        total = total + d_q[i]
    d_f[f] = total
    d_copies = spread(d_f, d_f_sem, "fsdp", f, F)

    def drain(slot, carry):
        for part in range(2):

            @pl.when((slot <= a) & has_right & (is_host | (slot == a)))
            def _():
                w_copy(wg.at[slot, part], slot, part, w_right, right).wait_send()

            @pl.when((slot >= a) & has_left & (is_host | (slot == a)))
            def _():
                w_copy(wg.at[slot, part], slot, part, w_left, left).wait_send()

        return carry

    lax.fori_loop(0, A, drain, 0)

    @pl.when(is_end)
    def _():
        for copy in [kg_end, pk_end] + x_end:
            copy.wait_send()

    for copy in kv_copies:
        copy.wait()
    totals = sequences(kv_f)
    by_query([total[:, :r] for total in totals], 0)
    by_query([total[:, r:] for total in totals], r * r)
    scores = score(0, 2 * r * r)
    for copy in d_copies:
        copy.wait()
    by_query(sequences(d_f), 2 * r * r)
    for seq, late_scores in enumerate(score(2 * r * r, r * r)):
        out_ref[pl.ds(seq, 1), :] = scores[seq] + late_scores


def shards(
    F,
    Q,
    resid_in,
    resid_grad,
    query_path_grad,
    hidden_act,
    key_grad,
    value_grad,
    key_weight,
    value_weight,
    norm_gain,
    proj_attn_in,
    proj_key_out,
    proj_value_out,
    proj_down_in,
    proj_down_out,
    query_grads,
    seq_counts,
):
    B = 2
    A = F // B
    t, d = resid_in.shape
    w = key_weight.shape[1]
    r = proj_attn_in.shape[0]
    seqs = seq_counts.shape[0]
    n = key_grad.shape[1] // (w * B)
    vmem = pl.BlockSpec(memory_space=pltpu.VMEM)
    hbm = pl.BlockSpec(memory_space=pl.ANY)
    dma = pltpu.SemaphoreType.DMA
    operands = (
        (resid_in, vmem),
        (resid_grad, hbm),
        (query_path_grad, hbm),
        (hidden_act, hbm),
        (key_grad, vmem),
        (value_grad, vmem),
        (key_weight, hbm),
        (value_weight, hbm),
        (norm_gain, vmem),
        (proj_attn_in, vmem),
        (proj_key_out, vmem),
        (proj_value_out, vmem),
        (proj_down_in, hbm),
        (proj_down_out, vmem),
        (query_grads, hbm),
        (seq_counts, pl.BlockSpec(memory_space=pltpu.SMEM)),
    )
    return pl.pallas_call(
        functools.partial(kernel, (F, Q, B, seqs)),
        out_shape=jax.ShapeDtypeStruct((seqs, query_grads.shape[0]), F32),
        in_specs=[spec for _, spec in operands],
        out_specs=vmem,
        scratch_shapes=[
            pltpu.VMEM(resid_grad.shape, BF16),
            pltpu.VMEM(query_path_grad.shape, BF16),
            pltpu.VMEM(hidden_act.shape, BF16),
            pltpu.VMEM(proj_down_in.shape, BF16),
            pltpu.VMEM(query_grads.shape, BF16),
            pltpu.VMEM((A, 2, d, w), BF16),
            pltpu.VMEM((2 * B * t + 2 * r, d), BF16),
            pltpu.VMEM((B, n, t, 2 * w), BF16),
            pltpu.VMEM((2, A, B * t, 2 * w), BF16),
            pltpu.VMEM((Q, t, 4 * r), F32),
            pltpu.VMEM((Q, 8, t), F32),
            pltpu.VMEM((2, B * t, 2 * r), F32),
            pltpu.VMEM((2, B * t, 2 * w), F32),
            pltpu.VMEM((2, B * t, r), F32),
            pltpu.VMEM((Q, r, 2 * r), F32),
            pltpu.VMEM((F, r, 2 * r), F32),
            pltpu.VMEM((Q, r, r), F32),
            pltpu.VMEM((F, r, r), F32),
            pltpu.VMEM((seqs, 8, 3 * r * r), F32),
            dma((7,)),
            dma((A, 2)),
            dma((A, 2)),
            dma((A, 2)),
            dma((2, B)),
            dma((2, CHUNKS)),
            dma((2, CHUNKS, B)),
            dma((2, B)),
            dma((2, Q)),
            dma((2,)),
            dma((2, Q)),
            dma((2, Q)),
            dma((2, Q)),
            dma((2, B)),
            dma((2,)),
            dma((2, B)),
            dma((2, Q)),
            dma((2, F)),
            dma((2, Q)),
            dma((2, F)),
        ],
        compiler_params=pltpu.CompilerParams(
            collective_id=0, has_side_effects=True, vmem_limit_bytes=56 * 2**20
        ),
    )(*(operand for operand, _ in operands))


def solution(mesh):
    placed = (
        P(("parts", "fsdp"), "query"),
        P(("parts", "fsdp"), "query"),
        P(("parts", "fsdp"), "query"),
        P(("parts", "fsdp"), "query"),
        P(("parts", "fsdp"), "query"),
        P(("parts", "fsdp"), "query"),
        P("query", "fsdp"),
        P("query", "fsdp"),
        P("query"),
        P(None, "query"),
        P(None, "query"),
        P(None, "query"),
        P(None, "query"),
        P(None, "query"),
        P(("fsdp", "query"), None),
        P("parts"),
    )
    return jax.shard_map(
        functools.partial(shards, mesh.shape["fsdp"], mesh.shape["query"]),
        mesh=mesh,
        in_specs=placed,
        out_specs=P("parts", ("fsdp", "query")),
        check_vma=False,
    )
```
